32 devices in a mesh: expert: 16 (over z, y, core), seq: 2 (over x).
Axes of the slice: x: 2, y: 2, z: 4, core: 2. Of those that a mesh axis runs over, the one named last changes fastest.
Arguments:
- tokens: bfloat16 [1536, 4096], P('expert', 'seq'), may hold values from -6 to 6
- cotangent: bfloat16 [1536, 4096], P('expert', 'seq'), may hold values from -0.59765625 to 0.59765625
- expert_ids: int32 [1536, 8], P('expert'), may hold values from 0 to 15, all different within a row; in each aligned block of 96 rows (0 to 95, 96 to 191, ...) at most 54 rows name the same one
- gate_values: bfloat16 [1536, 8], P('expert'), may hold values from 0.019897461 to 0.5
- gate_weight: bfloat16 [16, 4096, 768], P('expert', 'seq'), may hold values from -0.09375 to 0.09375
- up_weight: bfloat16 [16, 4096, 768], P('expert', 'seq'), may hold values from -0.09375 to 0.09375
- down_weight: bfloat16 [16, 768, 4096], P('expert', None, 'seq'), may hold values from -0.21875 to 0.21875
Outputs:
- input_grad: bfloat16 [1536, 4096], P('expert', 'seq')
- gate_grad: bfloat16 [1536, 8], P('expert')
- gate_weight_grad: bfloat16 [16, 4096, 768], P('expert', 'seq')
- up_weight_grad: bfloat16 [16, 4096, 768], P('expert', 'seq')
- down_weight_grad: bfloat16 [16, 768, 4096], P('expert', None, 'seq')
The draws below stay inside these ranges and needn't reach their ends.
Inputs may be any that keep to these rules, and one draw needn't show every extreme that they name: `expert_ids`: each row names 8 different experts; within each aligned block of 96 rows no expert is named by more than 54 rows, a bound that some block reaches.
All inputs are finite; a program needn't handle non-finite values.
Results may differ from the reference program's by a relative error of at most 0.019.
Values may be sent and summed in bfloat16 or wider, within the bound.
No kernel may reach another device: no remote copies, remote signals or barrier semaphores. Data moves between devices by JAX's collectives and lax.ppermute only.
A program may use at most 128 MiB of HBM per device.

```python
import math
import jax
import jax.numpy as jnp
import numpy as np
from jax import lax

D = 4096
HID = 768
TOPK = 8
TOK_GRP = 96
EXPERTS = 16
TOKENS = 1536
CAP = 54
ROWS = 864
N_EXPERT = 16
N_SEQ = 2


def block_levels(key, dims, shards, least, high):
    def one(axis_at, blocks):
        heights = jax.random.uniform(jax.random.fold_in(jax.random.fold_in(key, 6), axis_at), (blocks,), jnp.float32, least / len(shards), high / len(shards))
        return jnp.repeat(jnp.exp(heights), dims[axis_at] // blocks).reshape((-1,) + (1,) * (len(dims) - axis_at - 1))

    factor_of = one(*shards[0])
    for cut in shards[1:]:
        factor_of = factor_of * one(*cut)
    return factor_of


def routed_block(stream_key, own, number, rows, amount, top, reach, lean):
    ranking = jax.random.permutation(stream_key, amount)
    heavy_load, common = load_shares(amount, rows * top, reach, lean, True), load_shares(amount, rows * top, reach, lean, False)
    places = jnp.arange(amount)

    def named(sizes, turn):
        used = int((sizes > 0).sum())
        fixed = max(1, used // 4)
        moved = fixed + (places - fixed + turn * (used - fixed)) % max(1, amount - fixed)
        return jnp.zeros((amount,), jnp.int32).at[ranking[jnp.where(places < fixed, places, moved)]].set(jnp.asarray(sizes, jnp.int32))

    sizes = jnp.where(number % 4 == 0, named(heavy_load, number // 4), named(common, number - number // 4 - 1))
    mixed = jax.random.permutation(jax.random.fold_in(own, 3), amount)
    giver, sink = mixed[0:amount // 2 * 2:2], mixed[1:amount // 2 * 2:2]
    margin = jnp.minimum(sizes[giver] - 1, reach - sizes[sink]) // 2
    margin = jnp.where((giver == ranking[0]) | (sink == ranking[0]) | (sizes[sink] == 0), 0, jnp.maximum(margin, 0))
    moved = jax.random.randint(jax.random.fold_in(own, 4), (amount // 2,), 0, 1 << 20) % (margin + 1)
    sizes = sizes.at[giver].add(-moved).at[sink].add(moved)
    members = jnp.searchsorted(jnp.cumsum(sizes), jnp.arange(rows * top), side="right").astype(jnp.int32)
    table = members.reshape(top, rows).T
    table = table[jax.random.permutation(jax.random.fold_in(own, 1), rows)]
    turn = jax.random.randint(jax.random.fold_in(own, 2), (rows, 1), 0, top)
    return jnp.take_along_axis(table, (jnp.arange(top)[None, :] + turn) % top, axis=1)


def load_shares(number_of, total, most, lean, full):
    portions = [(1 << 20) // math.isqrt(grade ** lean) + 1 for grade in range(1, number_of + 1)]
    largest = most if full else min(most, max(-(-total // number_of), total * portions[0] // sum(portions)))
    least = 1 if total - largest >= number_of - 1 else 0
    holding, spare = [largest] + [least] * (number_of - 1), total - largest - least * (number_of - 1)
    while spare > 0:
        candidates = [i for i in range(1, number_of) if holding[i] < largest] or [i for i in range(1, number_of) if holding[i] < most]
        mass, budget = sum([portions[i] for i in candidates]), spare
        for i in candidates:
            extra = min(most - holding[i], max(1, budget * portions[i] // mass), spare)
            holding[i] = holding[i] + extra
            spare = spare - extra
    return np.array(holding)


def bell_draw(key, shape, width, reach, pieces=(), kind=jnp.bfloat16):
    level = block_levels(key, shape, pieces, -0.22, 0.18) if pieces else 1.0
    drawn = jax.random.normal(key, shape, jnp.float32) * width * level
    return jnp.minimum(jnp.maximum(drawn, -reach), reach).astype(kind)


def setup_inputs(seed: int = 0) -> dict:
    keys = jax.random.split(jax.random.key(seed), 8)
    tokens = bell_draw(keys[0], (TOKENS, D), 1.0, 6.0, ((0, 16), (1, 2)))
    cotangent = bell_draw(keys[1], (TOKENS, D), 0.1, 0.59765625, ((0, 16), (1, 2)))
    expert_ids_keys = jax.random.split(jax.random.fold_in(keys[2], 1), TOKENS // TOK_GRP)
    expert_ids_turns = jax.random.permutation(jax.random.fold_in(keys[2], 3), TOKENS // TOK_GRP)
    expert_ids = jax.vmap(lambda own, number: routed_block(jax.random.fold_in(keys[2], 2), own, number, TOK_GRP, EXPERTS, TOPK, CAP, 2))(expert_ids_keys, expert_ids_turns).reshape((TOKENS, TOPK))
    gate_values = jnp.clip(jnp.exp(math.log(0.5) - 3.224016 * jax.random.uniform(keys[3], (TOKENS, TOPK), jnp.float32) ** block_levels(keys[3], (TOKENS, TOPK), ((0, 16),), -0.2, 0.2)), 0.019897461, 0.5).astype(jnp.bfloat16)
    gate_weight = bell_draw(keys[4], (EXPERTS, D, HID), D ** -0.5, 0.09375, ((0, 16), (1, 2)))
    up_weight = bell_draw(keys[5], (EXPERTS, D, HID), D ** -0.5, 0.09375, ((0, 16), (1, 2)))
    down_weight = bell_draw(keys[6], (EXPERTS, HID, D), HID ** -0.5, 0.21875, ((0, 16), (2, 2)))
    return dict(tokens=tokens, cotangent=cotangent, expert_ids=expert_ids, gate_values=gate_values, gate_weight=gate_weight, up_weight=up_weight, down_weight=down_weight)


def pointwise(summed, gate_rows, hidden):
    gate_pre = summed[:, :hidden]
    up_pre = summed[:, hidden:2 * hidden]
    down_back = summed[:, 2 * hidden:]
    sigmoid_val = jax.nn.sigmoid(gate_pre)
    silu_val = gate_pre * sigmoid_val
    activation = silu_val * up_pre
    slot_grad = jnp.sum(activation * down_back, axis=-1)
    act_grad = gate_rows.astype(jnp.float32)[:, None] * down_back
    pre_gate_grad = act_grad * up_pre * sigmoid_val * (1.0 + gate_pre * (1.0 - sigmoid_val))
    pre_up_grad = act_grad * silu_val
    return (activation.astype(jnp.bfloat16), pre_gate_grad.astype(jnp.bfloat16),
            pre_up_grad.astype(jnp.bfloat16), slot_grad.astype(jnp.bfloat16))


def block_sum(parts):
    rounded = lax.optimization_barrier(parts.astype(jnp.bfloat16))
    return jnp.sum(rounded.astype(jnp.float32), axis=0)


def reference(tokens, cotangent, expert_ids, gate_values, gate_weight, up_weight, down_weight):
    quarter = D // N_SEQ
    grouped = expert_ids.reshape(N_EXPERT, TOK_GRP, TOPK)
    onehot = (grouped[..., None] == jnp.arange(EXPERTS, dtype=jnp.int32)).astype(jnp.int32)
    per_row = jnp.sum(onehot, axis=2)
    before = jnp.cumsum(per_row, axis=1) - per_row
    slot_index = jnp.sum(onehot * before[:, :, None, :], axis=3)
    group_number = jnp.arange(N_EXPERT, dtype=jnp.int32)[:, None, None]
    position = (grouped * ROWS + group_number * CAP + slot_index).reshape(-1)
    pair_number = jnp.arange(TOKENS * TOPK, dtype=jnp.int32)
    token_number = pair_number // TOPK
    token_of = jnp.full((EXPERTS * ROWS,), TOKENS, jnp.int32).at[position].set(token_number)
    pair_of = jnp.full((EXPERTS * ROWS,), TOKENS * TOPK, jnp.int32).at[position].set(pair_number)
    gate_of = jnp.zeros((EXPERTS * ROWS,), jnp.bfloat16).at[position].set(gate_values.reshape(-1))
    x_padded = jnp.concatenate([tokens, jnp.zeros((1, D), jnp.bfloat16)], axis=0)
    dy_padded = jnp.concatenate([cotangent, jnp.zeros((1, D), jnp.bfloat16)], axis=0)

    def one_expert(carry, inputs):
        dx_total, dg_total = carry
        token_rows, pair_rows, gate_rows, w_gate, w_up, w_down = inputs
        routed_x = x_padded[token_rows]
        routed_dy = dy_padded[token_rows]
        x_parts = routed_x.astype(jnp.float32).reshape(ROWS, N_SEQ, quarter)
        dy_parts = routed_dy.astype(jnp.float32).reshape(ROWS, N_SEQ, quarter)
        gate_pre = block_sum(jnp.einsum("rjd,jdh->jrh", x_parts, w_gate.astype(jnp.float32).reshape(N_SEQ, quarter, HID)))
        up_pre = block_sum(jnp.einsum("rjd,jdh->jrh", x_parts, w_up.astype(jnp.float32).reshape(N_SEQ, quarter, HID)))
        down_back = block_sum(jnp.einsum("rjd,hjd->jrh", dy_parts, w_down.astype(jnp.float32).reshape(HID, N_SEQ, quarter)))
        summed = jnp.concatenate([gate_pre, up_pre, down_back], axis=1)
        activation, pre_gate_grad, pre_up_grad, slot_grad = pointwise(summed, gate_rows, HID)
        scaled_dy = (gate_rows.astype(jnp.float32)[:, None] * routed_dy.astype(jnp.float32)).astype(jnp.bfloat16)
        down_grad = jnp.dot(activation.T, scaled_dy, preferred_element_type=jnp.float32).astype(jnp.bfloat16)
        gate_w_grad = jnp.dot(routed_x.T, pre_gate_grad, preferred_element_type=jnp.float32).astype(jnp.bfloat16)
        up_w_grad = jnp.dot(routed_x.T, pre_up_grad, preferred_element_type=jnp.float32).astype(jnp.bfloat16)
        row_grad = (jnp.dot(pre_gate_grad, w_gate.T, preferred_element_type=jnp.float32)
                    + jnp.dot(pre_up_grad, w_up.T, preferred_element_type=jnp.float32)).astype(jnp.bfloat16)
        dx_total = dx_total.at[token_rows].add(row_grad.astype(jnp.float32))
        dg_total = dg_total.at[pair_rows].set(slot_grad.astype(jnp.float32))
        return (dx_total, dg_total), (gate_w_grad, up_w_grad, down_grad)

    start = (jnp.zeros((TOKENS + 1, D), jnp.float32), jnp.zeros((TOKENS * TOPK + 1,), jnp.float32))
    inputs = (token_of.reshape(EXPERTS, ROWS), pair_of.reshape(EXPERTS, ROWS), gate_of.reshape(EXPERTS, ROWS),
              gate_weight, up_weight, down_weight)
    (dx_total, dg_total), (gate_w_all, up_w_all, down_all) = lax.scan(one_expert, start, inputs)
    input_grad = dx_total[:TOKENS].astype(jnp.bfloat16)
    gate_grad = dg_total[:TOKENS * TOPK].reshape(TOKENS, TOPK).astype(jnp.bfloat16)
    return (input_grad, gate_grad, gate_w_all, up_w_all, down_all)
```

```python
import functools

import jax
import jax.numpy as jnp
from jax import lax
from jax.experimental import pallas as pl
from jax.experimental.pallas import tpu as pltpu
from jax.sharding import PartitionSpec as P

BF = jnp.bfloat16
F32 = jnp.float32
LANES = 128
LAST = (((1,), (1,)), ((), ()))


def dot(a, b):
    return jnp.dot(a, b, preferred_element_type=F32)


def round_up(n, m):
    return -(-n // m) * m


def forward_kernel(inner, cap, tok, feat, hid, tile, *refs):
    blocks = refs[:inner]
    wg, wu, wd = refs[inner : inner + 3]
    parts, x_all, sd_all, st_out, grow_out = refs[-9:-4]
    cat, x_s, dy_s, lower = refs[-4:]
    rows = inner * cap
    pad = x_s.shape[0]
    step = pl.program_id(0)

    @pl.when(step == 0)
    def _():
        me = lax.axis_index("expert")
        mine = (lax.broadcasted_iota(jnp.int32, (tok, LANES), 1) == me).astype(F32)
        r = lax.broadcasted_iota(jnp.int32, (tok, tok), 0)
        c = lax.broadcasted_iota(jnp.int32, (tok, tok), 1)
        lower[...] = (c < r).astype(F32).astype(BF)
        slot_of = lax.broadcasted_iota(jnp.int32, (tok, pad), 1)
        st = []
        gates = []
        for b in range(inner):
            cat[b * tok : (b + 1) * tok, :] = blocks[b][:, : 2 * feat]
            table = blocks[b][:, 2 * feat :].astype(F32)
            gate = jnp.sum(table * mine, axis=1, keepdims=True)
            chosen = gate >= 0.0
            flag = jnp.broadcast_to(chosen.astype(F32), (tok, LANES))
            before = dot(lower[...], flag.astype(BF))[:, :1]
            place = jnp.where(chosen, before.astype(jnp.int32) + b * cap, -1)
            st.append((slot_of == place).astype(F32))
            gates.append(jnp.broadcast_to(gate, (tok, LANES)).astype(BF))
        st = jnp.concatenate(st, axis=0)
        gates = jnp.concatenate(gates, axis=0)
        st_out[...] = st.astype(BF)
        pick = st.T.astype(BF)
        grow = dot(pick, gates)
        grow_out[...] = grow.astype(BF)
        x = dot(pick, cat[:, :feat]).astype(BF)
        x_s[...] = x
        x_all[...] = x
        dy = dot(pick, cat[:, feat:])
        dy_s[...] = dy.astype(BF)
        sd_all[...] = (grow[:, :1] * dy).astype(BF)

    off = pl.multiple_of(step * tile, tile)
    parts[:, pl.ds(off, tile)] = dot(x_s[...], wg[...])[:rows].astype(BF)
    parts[:, pl.ds(hid + off, tile)] = dot(x_s[...], wu[...])[:rows].astype(BF)
    back = lax.dot_general(dy_s[...], wd[...], LAST, preferred_element_type=F32)
    parts[:, pl.ds(2 * hid + off, tile)] = back[:rows].astype(BF)


def forward_call(index, count, blocks, wg, wu, wd, cap, slabs):
    inner = len(blocks)
    tok = blocks[0].shape[0]
    feat, hid = wg.shape
    tile = 256 if hid % 256 == 0 else hid
    rows = inner * cap
    pad = round_up(rows, 16)
    whole = lambda shape: pl.BlockSpec(shape, lambda i: (0,) * len(shape))
    slab = lambda width: pl.BlockSpec((pad, width), lambda i: (index, 0))
    in_specs = [whole(b.shape) for b in blocks] + [
        pl.BlockSpec((feat, tile), lambda i: (0, i)),
        pl.BlockSpec((feat, tile), lambda i: (0, i)),
        pl.BlockSpec((tile, feat), lambda i: (i, 0)),
    ]
    args = list(blocks) + [wg, wu, wd]
    aliases = {}
    if slabs is not None:
        aliases = {len(args): 1, len(args) + 1: 2}
        args += list(slabs)
        in_specs += [pl.BlockSpec(memory_space=pl.ANY)] * 2
    return pl.pallas_call(
        functools.partial(forward_kernel, inner, cap, tok, feat, hid, tile),
        grid=(hid // tile,),
        in_specs=in_specs,
        out_specs=[
            whole((rows, 3 * hid)),
            slab(feat),
            slab(feat),
            whole((inner * tok, pad)),
            whole((pad, LANES)),
        ],
        out_shape=[
            jax.ShapeDtypeStruct((rows, 3 * hid), BF),
            jax.ShapeDtypeStruct((count * pad, feat), BF),
            jax.ShapeDtypeStruct((count * pad, feat), BF),
            jax.ShapeDtypeStruct((inner * tok, pad), BF),
            jax.ShapeDtypeStruct((pad, LANES), BF),
        ],
        scratch_shapes=[
            pltpu.VMEM((inner * tok, 2 * feat), BF),
            pltpu.VMEM((pad, feat), BF),
            pltpu.VMEM((pad, feat), BF),
            pltpu.VMEM((tok, tok), BF),
        ],
        input_output_aliases=aliases,
        compiler_params=pltpu.CompilerParams(vmem_limit_bytes=40 * 1024 * 1024),
        cost_estimate=pl.CostEstimate(
            flops=6 * pad * feat * hid + 4 * pad * inner * tok * feat,
            bytes_accessed=2 * (3 * feat * hid + 2 * inner * tok * feat + 2 * pad * feat + 3 * pad * hid),
            transcendentals=0,
        ),
    )(*args)


def backward_kernel(inner, tok, feat, hid, tile, n_parts, *refs):
    parts = refs[:n_parts]
    st, grow, wg, wu = refs[n_parts : n_parts + 4]
    keep, send, act_all, pg_all, pu_all = refs[-7:-2]
    pg_s, pu_s = refs[-2:]
    rows = parts[0].shape[0]
    pad = pg_s.shape[0]
    half = inner // 2
    step = pl.program_id(0)

    def spread(value, column, width):
        for b in range(inner):
            piece = value[b * tok : (b + 1) * tok]
            target = keep if b % 2 == 0 else send
            target[b // 2, :, pl.ds(column, width)] = piece

    @pl.when(step == 0)
    def _():
        def total(at):
            out = parts[0][:, at * hid : (at + 1) * hid].astype(F32)
            for part in parts[1:]:
                out = out + part[:, at * hid : (at + 1) * hid].astype(F32)
            return out

        def full(value):
            if pad > rows:
                value = jnp.concatenate([value, jnp.zeros((pad - rows, value.shape[1]), F32)], axis=0)
            return value

        gate_pre = total(0)
        sig = 1.0 / (1.0 + jnp.exp(-gate_pre))
        silu = gate_pre * sig
        up = total(1)
        act = silu * up
        back = total(2)
        slot = jnp.sum(act * back, axis=1, keepdims=True)
        act_grad = grow[:rows, :1].astype(F32) * back
        pre_gate = act_grad * up * sig * (1.0 + gate_pre * (1.0 - sig))
        pre_up = act_grad * silu
        act_all[...] = full(act).astype(BF)
        pg = full(pre_gate).astype(BF)
        pu = full(pre_up).astype(BF)
        pg_all[...] = pg
        pu_all[...] = pu
        pg_s[...] = pg
        pu_s[...] = pu
        me = lax.axis_index("expert")
        mine = (lax.broadcasted_iota(jnp.int32, (rows, LANES), 1) == me).astype(F32)
        slots = full(slot * mine).astype(BF)
        spread(dot(st[...], slots).astype(BF), feat, LANES)

    off = pl.multiple_of(step * tile, tile)
    grad = lax.dot_general(pg_s[...], wg[...], LAST, preferred_element_type=F32)
    grad = grad + lax.dot_general(pu_s[...], wu[...], LAST, preferred_element_type=F32)
    spread(dot(st[...], grad.astype(BF)).astype(BF), off, tile)


def backward_call(index, count, parts, st, grow, wg, wu, tok, slabs):
    feat, hid = wg.shape
    tile = 512 if feat % 512 == 0 else feat
    inner = st.shape[0] // tok
    pad = st.shape[1]
    rows = parts[0].shape[0]
    wide = feat + LANES
    whole = lambda shape: pl.BlockSpec(shape, lambda i: (0,) * len(shape))
    slab = pl.BlockSpec((pad, hid), lambda i: (index, 0))
    weight = pl.BlockSpec((tile, hid), lambda i: (i, 0))
    args = list(parts) + [st, grow, wg, wu]
    in_specs = [whole(a.shape) for a in args[:-2]] + [weight, weight]
    aliases = {}
    if slabs is not None:
        aliases = {len(args) + i: 2 + i for i in range(3)}
        args += list(slabs)
        in_specs += [pl.BlockSpec(memory_space=pl.ANY)] * 3
    half = jax.ShapeDtypeStruct((inner // 2, tok, wide), BF)
    saved = jax.ShapeDtypeStruct((count * pad, hid), BF)
    return pl.pallas_call(
        functools.partial(backward_kernel, inner, tok, feat, hid, tile, len(parts)),
        grid=(feat // tile,),
        in_specs=in_specs,
        out_specs=[whole(half.shape), whole(half.shape), slab, slab, slab],
        out_shape=[half, half, saved, saved, saved],
        scratch_shapes=[pltpu.VMEM((pad, hid), BF), pltpu.VMEM((pad, hid), BF)],
        input_output_aliases=aliases,
        compiler_params=pltpu.CompilerParams(vmem_limit_bytes=40 * 1024 * 1024),
        cost_estimate=pl.CostEstimate(
            flops=4 * pad * feat * hid + 2 * pad * inner * tok * feat,
            bytes_accessed=2 * (2 * feat * hid + inner * tok * feat + 9 * pad * hid),
            transcendentals=pad * hid,
        ),
    )(*args)


def local(tokens, cotangent, expert_ids, gate_values, gate_weight, up_weight, down_weight):
    experts = lax.axis_size("expert")
    seqs = lax.axis_size("seq")
    tok, feat = tokens.shape
    top = expert_ids.shape[1]
    cap = min(tok, tok * top // experts + tok * top // (8 * experts))
    inner = 2 * seqs if experts % (2 * seqs) == 0 else 2
    columns = inner // 2
    planes = experts // inner

    def split(i):
        return i // inner, (i % inner) // 2, i % 2

    def join(z, y, c):
        return (z % planes) * inner + (y % columns) * 2 + c

    def shift(dz=0, dy=0, dc=0):
        out = []
        for i in range(experts):
            z, y, c = split(i)
            out.append((i, join(z + dz, y + dy, c ^ dc)))
        return out

    def move(x, **by):
        return lax.ppermute(x, "expert", shift(**by))

    wg, wu, wd = gate_weight[0], up_weight[0], down_weight[0]
    lanes = jnp.arange(LANES, dtype=jnp.int32)
    hit = expert_ids[:, :, None] == lanes
    chosen = jnp.any(hit, axis=1)
    table = jnp.sum(jnp.where(hit, gate_values[:, :, None].astype(F32), 0.0), axis=1)
    table = jnp.where(chosen, table, -1.0).astype(BF)
    block = jnp.concatenate([tokens, cotangent, table], axis=1)

    planes_in = [block] + [move(block, dz=k) for k in range(1, planes)]
    x_slab = act_slab = None
    totals = None
    for k in range(planes):
        mine = [planes_in[k]] + [move(planes_in[k], dy=j) for j in range(1, columns)]
        theirs = [move(b, dc=1) for b in mine]
        blocks = [b for pair in zip(mine, theirs) for b in pair]
        part, xs, sds, st, grow = forward_call(k, planes, blocks, wg, wu, wd, cap, x_slab)
        x_slab = (xs, sds)
        if seqs == 2:
            parts = [part, lax.ppermute(part, "seq", [(0, 1), (1, 0)])]
        else:
            gathered = lax.all_gather(part, "seq", axis=0)
            parts = [gathered[i] for i in range(seqs)]
        keep, send, *act_slab = backward_call(k, planes, parts, st, grow, wg, wu, tok, act_slab)
        got = move(send, dc=1)
        both = (keep.astype(F32) + got.astype(F32)).astype(BF)
        summed = both[0].astype(F32)
        for j in range(1, columns):
            summed = summed + move(both[j], dy=-j).astype(F32)
        if k:
            summed = move(summed.astype(BF), dz=-k).astype(F32)
        totals = summed if totals is None else totals + summed

    input_grad = totals[:, :feat].astype(BF)
    slots = totals[:, feat:]
    gate_grad = jnp.sum(jnp.where(hit, slots[:, None, :], 0.0), axis=2).astype(BF)
    contract_rows = (((0,), (0,)), ((), ()))
    wgrad = lambda a, b: lax.dot_general(a, b, contract_rows, preferred_element_type=F32).astype(BF)[None]
    x_all, sd_all = x_slab
    act_all, pg_all, pu_all = act_slab
    return (
        input_grad,
        gate_grad,
        wgrad(x_all, pg_all),
        wgrad(x_all, pu_all),
        wgrad(act_all, sd_all),
    )


def solution(mesh):
    in_specs = (
        P("expert", "seq"),
        P("expert", "seq"),
        P("expert", None),
        P("expert", None),
        P("expert", "seq", None),
        P("expert", "seq", None),
        P("expert", None, "seq"),
    )
    out_specs = (
        P("expert", "seq"),
        P("expert", None),
        P("expert", "seq", None),
        P("expert", "seq", None),
        P("expert", None, "seq"),
    )
    return jax.shard_map(local, mesh=mesh, in_specs=in_specs, out_specs=out_specs, check_vma=False)
```

```python
import functools

import jax
import jax.numpy as jnp
from jax import lax
from jax.experimental import pallas as pl
from jax.experimental.pallas import tpu as pltpu
from jax.sharding import PartitionSpec as P

BF = jnp.bfloat16
F32 = jnp.float32
LANES = 128
VMEM_LIMIT = 30 * 1024 * 1024
LAST = (((1,), (1,)), ((), ()))


def dot(a, b):
    return jnp.dot(a, b, preferred_element_type=F32)


def round_up(n, m):
    return -(-n // m) * m


def forward_kernel(inner, cap, tok, feat, hid, tile, *refs):
    blocks = refs[:inner]
    wg, wu, wd = refs[inner : inner + 3]
    parts, x_all, sd_all, st_out, grow_out = refs[-9:-4]
    cat, x_s, dy_s, lower = refs[-4:]
    rows = inner * cap
    pad = x_s.shape[0]
    step = pl.program_id(0)

    @pl.when(step == 0)
    def _():
        me = lax.axis_index("expert")
        mine = (lax.broadcasted_iota(jnp.int32, (tok, LANES), 1) == me).astype(F32)
        r = lax.broadcasted_iota(jnp.int32, (tok, tok), 0)
        c = lax.broadcasted_iota(jnp.int32, (tok, tok), 1)
        lower[...] = (c < r).astype(F32).astype(BF)
        slot_of = lax.broadcasted_iota(jnp.int32, (tok, pad), 1)
        st = []
        gates = []
        for b in range(inner):
            cat[b * tok : (b + 1) * tok, :] = blocks[b][:, : 2 * feat]
            table = blocks[b][:, 2 * feat :].astype(F32)
            gate = jnp.sum(table * mine, axis=1, keepdims=True)
            chosen = gate >= 0.0
            flag = jnp.broadcast_to(chosen.astype(F32), (tok, LANES))
            before = dot(lower[...], flag.astype(BF))[:, :1]
            place = jnp.where(chosen, before.astype(jnp.int32) + b * cap, -1)
            st.append((slot_of == place).astype(F32))
            gates.append(jnp.broadcast_to(gate, (tok, LANES)).astype(BF))
        st = jnp.concatenate(st, axis=0)
        gates = jnp.concatenate(gates, axis=0)
        st_out[...] = st.astype(BF)
        pick = st.T.astype(BF)
        grow = dot(pick, gates)
        grow_out[...] = grow.astype(BF)
        x = dot(pick, cat[:, :feat]).astype(BF)
        x_s[...] = x
        x_all[...] = x
        dy = dot(pick, cat[:, feat:])
        dy_s[...] = dy.astype(BF)
        sd_all[...] = (grow[:, :1] * dy).astype(BF)

    off = pl.multiple_of(step * tile, tile)
    cols = pl.ds(off, tile)
    parts[:, cols] = dot(x_s[...], wg[:, cols])[:rows].astype(BF)
    parts[:, pl.ds(hid + off, tile)] = dot(x_s[...], wu[:, cols])[:rows].astype(BF)
    back = lax.dot_general(dy_s[...], wd[cols, :], LAST, preferred_element_type=F32)
    parts[:, pl.ds(2 * hid + off, tile)] = back[:rows].astype(BF)


COST = pl.CostEstimate(flops=1000, bytes_accessed=1000, transcendentals=0)
ANY = pl.BlockSpec(memory_space=pl.ANY)
VMEM = pl.BlockSpec(memory_space=pltpu.VMEM)


def in_hbm(arrays):
    return [pltpu.with_memory_space_constraint(x, pltpu.HBM) for x in arrays]


def in_vmem(arrays):
    return [pltpu.with_memory_space_constraint(x, pltpu.VMEM) for x in arrays]


def tie(x, *after):
    return pl.pallas_call(
        lambda *refs: None,
        in_specs=[ANY] * (1 + len(after)),
        out_specs=ANY,
        out_shape=jax.ShapeDtypeStruct(x.shape, x.dtype),
        input_output_aliases={0: 0},
        compiler_params=pltpu.CompilerParams(vmem_limit_bytes=1024 * 1024),
        cost_estimate=COST,
    )(x, *in_hbm(after))


def block_kernel(tokens, cotangent, ids, gates, out):
    tok, feat = tokens.shape
    out[:, :feat] = tokens[...]
    out[:, feat : 2 * feat] = cotangent[...]
    expert = lax.broadcasted_iota(jnp.int32, (LANES, tok), 0)
    table = jnp.full((LANES, tok), -1.0, F32)
    for k in range(ids.shape[0]):
        table = jnp.where(expert == ids[k : k + 1, :], gates[k : k + 1, :].astype(F32), table)
    out[:, 2 * feat :] = table.T.astype(BF)


def make_block(tokens, cotangent, ids, gates):
    tok, feat = tokens.shape
    return pl.pallas_call(
        block_kernel,
        out_shape=jax.ShapeDtypeStruct((tok, 2 * feat + LANES), BF),
        compiler_params=pltpu.CompilerParams(vmem_limit_bytes=VMEM_LIMIT),
        cost_estimate=COST,
    )(*in_hbm([tokens, cotangent, ids.T, gates.T]))


def forward_kernel(cfg, *refs):
    inner, cap, tok, feat, hid, tile, fresh, n_after, n_slabs, n_add = cfg
    refs = list(refs)

    def take(n):
        out = refs[:n]
        del refs[:n]
        return out

    blocks = take(inner)
    weights = take(3)
    take(n_after + n_slabs)
    added = take(2 if n_add else 0)
    parts, x_all, sd_all, st_out, grow_out, token = take(6)
    sums = take(n_add)
    held = take(3 if fresh else 0)
    cat, x_s, dy_s, lower, *sems = refs
    rows = inner * cap
    pad = x_s.shape[0]
    step = pl.program_id(0)
    off = pl.multiple_of(step * tile, tile)
    cols = pl.ds(off, tile)

    def fetch(i, at):
        cut = (at, slice(None)) if i == 2 else (slice(None), at)
        return pltpu.make_async_copy(weights[i].at[cut], held[i].at[cut], sems[0].at[i])

    @pl.when(step == 0)
    def _():
        if fresh:
            for i in range(3):
                fetch(i, pl.ds(0, tile)).start()
        me = lax.axis_index("expert")
        mine = (lax.broadcasted_iota(jnp.int32, (tok, LANES), 1) == me).astype(F32)
        r = lax.broadcasted_iota(jnp.int32, (tok, tok), 0)
        c = lax.broadcasted_iota(jnp.int32, (tok, tok), 1)
        lower[...] = (c < r).astype(F32).astype(BF)
        slot_of = lax.broadcasted_iota(jnp.int32, (tok, pad), 1)
        st = []
        gates = []
        for b in range(inner):
            cat[b * tok : (b + 1) * tok, :] = blocks[b][:, : 2 * feat]
            table = blocks[b][:, 2 * feat :].astype(F32)
            gate = jnp.sum(table * mine, axis=1, keepdims=True)
            chosen = gate >= 0.0
            flag = jnp.broadcast_to(chosen.astype(F32), (tok, LANES))
            before = dot(lower[...], flag.astype(BF))[:, :1]
            place = jnp.where(chosen, before.astype(jnp.int32) + b * cap, -1)
            st.append((slot_of == place).astype(F32))
            gates.append(jnp.broadcast_to(gate, (tok, LANES)).astype(BF))
        st = jnp.concatenate(st, axis=0)
        gates = jnp.concatenate(gates, axis=0)
        st_out[...] = st.astype(BF)
        pick = st.T.astype(BF)
        grow = dot(pick, gates)
        grow_out[...] = grow.astype(BF)
        x = dot(pick, cat[:, :feat]).astype(BF)
        x_s[...] = x
        x_all[...] = x
        dy = dot(pick, cat[:, feat:])
        dy_s[...] = dy.astype(BF)
        sd_all[...] = (grow[:, :1] * dy).astype(BF)
        token[...] = jnp.zeros_like(token)
        for i in range(n_add):
            sums[i][...] = (added[0][i].astype(F32) + added[1][i].astype(F32)).astype(BF)

    if fresh:
        for i in range(3):
            fetch(i, cols).wait()

        @pl.when(step + 1 < hid // tile)
        def _():
            for i in range(3):
                fetch(i, pl.ds(pl.multiple_of((step + 1) * tile, tile), tile)).start()

        weights = held
    wg, wu, wd = weights
    parts[:, cols] = dot(x_s[...], wg[:, cols])[:rows].astype(BF)
    parts[:, pl.ds(hid + off, tile)] = dot(x_s[...], wu[:, cols])[:rows].astype(BF)
    back = lax.dot_general(dy_s[...], wd[cols, :], LAST, preferred_element_type=F32)
    parts[:, pl.ds(2 * hid + off, tile)] = back[:rows].astype(BF)


def forward_call(start, total, pad, blocks, weights, fresh, cap, slabs, after, added):
    inner = len(blocks)
    tok = blocks[0].shape[0]
    feat, hid = weights[0].shape
    tile = 256 if hid % 256 == 0 else hid
    rows = inner * cap
    index = start // (inner // 2)
    whole = lambda shape: pl.BlockSpec(shape, lambda i: (0,) * len(shape))
    slab = lambda width: pl.BlockSpec((pad, width), lambda i: (index, 0))
    n_add = added[0].shape[0] if added else 0
    in_specs = [whole(b.shape) for b in blocks] + [ANY if fresh else VMEM] * 3 + [ANY] * (len(after) + len(slabs))
    args = list(blocks) + (in_hbm(weights) if fresh else in_vmem(weights)) + in_hbm(after)
    aliases = {len(args) + i: 1 + i for i in range(len(slabs))}
    args += [*slabs, *in_hbm(added[:1]), *added[1:]]
    in_specs += [whole(a.shape) for a in added]
    out_specs = [
        whole((rows, 3 * hid)),
        slab(feat),
        slab(feat),
        whole((inner * tok, pad)),
        whole((pad, LANES)),
        whole((8, LANES)),
    ]
    out_shape = [
        pltpu.HBM((rows, 3 * hid), BF),
        pltpu.HBM((total, feat), BF),
        pltpu.HBM((total, feat), BF),
        pltpu.HBM((inner * tok, pad), BF),
        pltpu.HBM((pad, LANES), BF),
        pltpu.HBM((8, LANES), F32),
    ]
    for i in range(n_add):
        out_specs.append(whole(added[0].shape[1:]))
        out_shape.append(pltpu.HBM(added[0].shape[1:], BF))
    scratch = [
        pltpu.VMEM((inner * tok, 2 * feat), BF),
        pltpu.VMEM((pad, feat), BF),
        pltpu.VMEM((pad, feat), BF),
        pltpu.VMEM((tok, tok), BF),
    ]
    if fresh:
        out_specs += [VMEM] * 3
        out_shape += [pltpu.VMEM(w.shape, w.dtype) for w in weights]
        scratch.append(pltpu.SemaphoreType.DMA((3,)))
    cfg = (inner, cap, tok, feat, hid, tile, fresh, len(after), len(slabs), n_add)
    out = pl.pallas_call(
        functools.partial(forward_kernel, cfg),
        grid=(hid // tile,),
        in_specs=in_specs,
        out_specs=out_specs,
        out_shape=out_shape,
        scratch_shapes=scratch,
        input_output_aliases=aliases,
        compiler_params=pltpu.CompilerParams(vmem_limit_bytes=VMEM_LIMIT),
        cost_estimate=COST,
    )(*args)
    return out[:6], out[6 : 6 + n_add], out[6 + n_add :]


def backward_kernel(inner, tok, feat, hid, tile, n_parts, *refs):
    parts = refs[:n_parts]
    st, grow, wg, wu = refs[n_parts : n_parts + 4]
    keep, send, act_all, pg_all, pu_all, token = refs[-8:-2]
    pg_s, pu_s = refs[-2:]
    rows = parts[0].shape[0]
    pad = pg_s.shape[0]
    half = inner // 2
    step = pl.program_id(0)

    def spread(value, column, width):
        for b in range(inner):
            piece = value[b * tok : (b + 1) * tok]
            target = keep if b % 2 == 0 else send
            target[b // 2, :, pl.ds(column, width)] = piece

    @pl.when(step == 0)
    def _():
        def total(at):
            out = parts[0][:, at * hid : (at + 1) * hid].astype(F32)
            for part in parts[1:]:
                out = out + part[:, at * hid : (at + 1) * hid].astype(F32)
            return out

        def full(value):
            if pad > rows:
                value = jnp.concatenate([value, jnp.zeros((pad - rows, value.shape[1]), F32)], axis=0)
            return value

        gate_pre = total(0)
        sig = 1.0 / (1.0 + jnp.exp(-gate_pre))
        silu = gate_pre * sig
        up = total(1)
        act = silu * up
        back = total(2)
        slot = jnp.sum(act * back, axis=1, keepdims=True)
        act_grad = grow[:rows, :1].astype(F32) * back
        pre_gate = act_grad * up * sig * (1.0 + gate_pre * (1.0 - sig))
        pre_up = act_grad * silu
        token[...] = jnp.zeros_like(token)
        act_all[...] = full(act).astype(BF)
        pg = full(pre_gate).astype(BF)
        pu = full(pre_up).astype(BF)
        pg_all[...] = pg
        pu_all[...] = pu
        pg_s[...] = pg
        pu_s[...] = pu
        me = lax.axis_index("expert")
        mine = (lax.broadcasted_iota(jnp.int32, (rows, LANES), 1) == me).astype(F32)
        slots = full(slot * mine).astype(BF)
        spread(dot(st[...], slots).astype(BF), feat, LANES)

    off = pl.multiple_of(step * tile, tile)
    cut = pl.ds(off, tile)
    grad = lax.dot_general(pg_s[...], wg[cut, :], LAST, preferred_element_type=F32)
    grad = grad + lax.dot_general(pu_s[...], wu[cut, :], LAST, preferred_element_type=F32)
    spread(dot(st[...], grad.astype(BF)).astype(BF), off, tile)


def backward_call(start, total, pad, parts, st, grow, wg, wu, tok, slabs, after):
    feat, hid = wg.shape
    tile = 512 if feat % 512 == 0 else feat
    inner = st.shape[0] // tok
    rows = parts[0].shape[0]
    index = start // (inner // 2)
    wide = feat + LANES
    whole = lambda shape: pl.BlockSpec(shape, lambda i: (0,) * len(shape))
    slab = pl.BlockSpec((pad, hid), lambda i: (index, 0))
    args = in_hbm(parts[:1]) + list(parts[1:]) + in_hbm([st, grow]) + in_vmem([wg, wu]) + in_hbm(after)
    in_specs = [whole(a.shape) for a in args[: len(parts) + 2]] + [VMEM] * 2 + [ANY] * len(after)
    aliases = {}
    if slabs:
        aliases = {len(args) + i: 2 + i for i in range(3)}
        args += list(slabs)
        in_specs += [ANY] * 3
    half = pltpu.HBM((inner // 2, tok, wide), BF)
    saved = pltpu.HBM((total, hid), BF)
    return pl.pallas_call(
        functools.partial(backward_kernel, inner, tok, feat, hid, tile, len(parts)),
        grid=(feat // tile,),
        in_specs=in_specs,
        out_specs=[whole(half.shape), whole(half.shape), slab, slab, slab, whole((8, LANES))],
        out_shape=[half, half, saved, saved, saved, pltpu.HBM((8, LANES), F32)],
        scratch_shapes=[pltpu.VMEM((pad, hid), BF), pltpu.VMEM((pad, hid), BF)],
        input_output_aliases=aliases,
        compiler_params=pltpu.CompilerParams(vmem_limit_bytes=VMEM_LIMIT),
        cost_estimate=COST,
    )(*args)


def local(tokens, cotangent, expert_ids, gate_values, gate_weight, up_weight, down_weight):
    experts = lax.axis_size("expert")
    seqs = lax.axis_size("seq")
    tok, feat = tokens.shape
    top = expert_ids.shape[1]
    cap = min(tok, tok * top // experts + tok * top // (8 * experts))
    inner = 2 * seqs if experts % (2 * seqs) == 0 else 2
    columns = inner // 2
    planes = experts // inner

    def split(i):
        return i // inner, (i % inner) // 2, i % 2

    def join(z, y, c):
        return (z % planes) * inner + (y % columns) * 2 + c

    def shift(dz=0, dy=0, dc=0):
        out = []
        for i in range(experts):
            z, y, c = split(i)
            out.append((i, join(z + dz, y + dy, c ^ dc)))
        return out

    def move(x, **by):
        return lax.ppermute(x, "expert", shift(**by))

    wg, wu, wd = gate_weight[0], up_weight[0], down_weight[0]
    hit = expert_ids[:, :, None] == jnp.arange(LANES, dtype=jnp.int32)
    block = make_block(tokens, cotangent, expert_ids, gate_values)

    def swap(part):
        if seqs == 2:
            return [part, lax.ppermute(part, "seq", [(0, 1), (1, 0)])]
        gathered = lax.all_gather(part, "seq", axis=0)
        return [gathered[i] for i in range(seqs)]

    order = list(range(planes // 2 + 1)) + list(range(planes - 1, planes // 2, -1))
    pieces = [(k, j) for k in order for j in range(columns)]
    ends = [1 + columns * i for i in range(planes)]
    ends += [ends[-1] + i for i in range(1, columns)]
    chunks = [pieces[lo:hi] for lo, hi in zip([0] + ends, ends)]
    unit = round_up(2 * cap, 16)
    total_rows = planes * columns * unit
    starts, at = [0] * len(chunks), 0
    for size in sorted({len(c) for c in chunks}, reverse=True):
        for n, chunk in enumerate(chunks):
            if len(chunk) == size:
                starts[n], at = at, at + size

    arrived = {(0, 0): block}
    pending = {}

    def send_on(k):
        own = arrived[k, 0]
        for j in range(1, columns):
            pending[k, j] = move(own, dy=j)
        if k < planes - k and k + 1 <= planes // 2:
            pending[k + 1, 0] = move(own, dz=1)
        if k == 0 and planes > 2:
            pending[planes - 1, 0] = move(own, dz=-1)
        elif planes - k < k and planes - k + 1 < (planes + 1) // 2:
            pending[k - 1, 0] = move(own, dz=-1)

    send_on(0)
    x_slab = act_slab = ()
    returned = {}
    outgoing = {}
    totals = []

    def finish(entry, after):
        nonlocal act_slab
        start, chunk, parts, st, grow = entry
        keep, send, *act_slab, token = backward_call(
            start, total_rows, len(chunk) * unit, parts, st, grow, *held[:2], tok, act_slab, after
        )
        return token, (keep, move(send, dc=1))

    def add(keep, got):
        return [(keep[i].astype(F32) + got[i].astype(F32)).astype(BF) for i in range(keep.shape[0])]

    def give_back(chunk, sums):
        for (k, j), value in zip(chunk, sums):
            returned[k, j] = move(value, dy=-j) if j else value
        for k in {k: None for k, _ in chunk}:
            if all((k, j) in returned for j in range(columns)):
                summed = sum(returned[k, j].astype(F32) for j in range(columns))
                if k:
                    outgoing[k] = summed.astype(BF)
                    summed = move(outgoing[k], dz=-k).astype(F32)
                totals.append(summed)

    held = (wg, wu, wd)
    entries, unsent = [], []
    sent = token = None
    for n, chunk in enumerate(chunks):
        blocks = []
        for piece in chunk:
            if piece not in arrived:
                arrived[piece] = tie(pending.pop(piece), token)
                if piece[1] == 0:
                    send_on(piece[0])
            blocks += [arrived[piece], move(arrived[piece], dc=1)]
        added = unsent.pop(0) if unsent else None
        (part, *x_slab, st, grow, sent), sums, loaded = forward_call(
            starts[n], total_rows, len(chunk) * unit, blocks, held, n == 0, cap, x_slab,
            [] if token is None else [token], added[1] if added else ()
        )
        held = loaded or held
        if added:
            give_back(added[0], sums)
        entries.append((starts[n], chunk, swap(part), st, grow))
        if n != 1:
            done = entries.pop(0)
            token, halves = finish(done, [sent])
            unsent.append((done[1], halves))
    for last_chunk, halves in unsent:
        sums = add(*halves)
        give_back(last_chunk, sums)
    done = entries.pop(0)
    token, halves = finish(done, [token, *sums])
    sums = add(*halves)
    give_back(done[1], sums)

    totals = sum(totals[1:], totals[0])
    input_grad = totals[:, :feat].astype(BF)
    slots = totals[:, feat:]
    gate_grad = jnp.sum(jnp.where(hit, slots[:, None, :], 0.0), axis=2).astype(BF)
    contract_rows = (((0,), (0,)), ((), ()))
    wgrad = lambda a, b: lax.dot_general(a, b, contract_rows, preferred_element_type=F32).astype(BF)[None]
    x_all, sd_all = x_slab
    act_all, pg_all, pu_all = act_slab
    leaving = list(outgoing.values())
    down = wgrad(act_all, tie(sd_all, *sums, *leaving[:-1]))
    x_all = tie(x_all, *leaving)
    return (
        input_grad,
        gate_grad,
        wgrad(x_all, pg_all),
        wgrad(x_all, pu_all),
        down,
    )


def solution(mesh):
    in_specs = (
        P("expert", "seq"),
        P("expert", "seq"),
        P("expert", None),
        P("expert", None),
        P("expert", "seq", None),
        P("expert", "seq", None),
        P("expert", None, "seq"),
    )
    out_specs = (
        P("expert", "seq"),
        P("expert", None),
        P("expert", "seq", None),
        P("expert", "seq", None),
        P("expert", None, "seq"),
    )
    return jax.shard_map(local, mesh=mesh, in_specs=in_specs, out_specs=out_specs, check_vma=False)
```

```python
import functools

import jax
import jax.numpy as jnp
from jax import lax
from jax.experimental import pallas as pl
from jax.experimental.pallas import tpu as pltpu
from jax.sharding import PartitionSpec as P

BF = jnp.bfloat16
F32 = jnp.float32
LANES = 128
VMEM_LIMIT = 30 * 1024 * 1024
LAST = (((1,), (1,)), ((), ()))


def dot(a, b):
    return jnp.dot(a, b, preferred_element_type=F32)


def round_up(n, m):
    return -(-n // m) * m


def forward_kernel(inner, cap, tok, feat, hid, tile, *refs):
    blocks = refs[:inner]
    wg, wu, wd = refs[inner : inner + 3]
    parts, x_all, sd_all, st_out, grow_out = refs[-9:-4]
    cat, x_s, dy_s, lower = refs[-4:]
    rows = inner * cap
    pad = x_s.shape[0]
    step = pl.program_id(0)

    @pl.when(step == 0)
    def _():
        me = lax.axis_index("expert")
        mine = (lax.broadcasted_iota(jnp.int32, (tok, LANES), 1) == me).astype(F32)
        r = lax.broadcasted_iota(jnp.int32, (tok, tok), 0)
        c = lax.broadcasted_iota(jnp.int32, (tok, tok), 1)
        lower[...] = (c < r).astype(F32).astype(BF)
        slot_of = lax.broadcasted_iota(jnp.int32, (tok, pad), 1)
        st = []
        gates = []
        for b in range(inner):
            cat[b * tok : (b + 1) * tok, :] = blocks[b][:, : 2 * feat]
            table = blocks[b][:, 2 * feat :].astype(F32)
            gate = jnp.sum(table * mine, axis=1, keepdims=True)
            chosen = gate >= 0.0
            flag = jnp.broadcast_to(chosen.astype(F32), (tok, LANES))
            before = dot(lower[...], flag.astype(BF))[:, :1]
            place = jnp.where(chosen, before.astype(jnp.int32) + b * cap, -1)
            st.append((slot_of == place).astype(F32))
            gates.append(jnp.broadcast_to(gate, (tok, LANES)).astype(BF))
        st = jnp.concatenate(st, axis=0)
        gates = jnp.concatenate(gates, axis=0)
        st_out[...] = st.astype(BF)
        pick = st.T.astype(BF)
        grow = dot(pick, gates)
        grow_out[...] = grow.astype(BF)
        x = dot(pick, cat[:, :feat]).astype(BF)
        x_s[...] = x
        x_all[...] = x
        dy = dot(pick, cat[:, feat:])
        dy_s[...] = dy.astype(BF)
        sd_all[...] = (grow[:, :1] * dy).astype(BF)

    off = pl.multiple_of(step * tile, tile)
    cols = pl.ds(off, tile)
    parts[:, cols] = dot(x_s[...], wg[:, cols])[:rows].astype(BF)
    parts[:, pl.ds(hid + off, tile)] = dot(x_s[...], wu[:, cols])[:rows].astype(BF)
    back = lax.dot_general(dy_s[...], wd[cols, :], LAST, preferred_element_type=F32)
    parts[:, pl.ds(2 * hid + off, tile)] = back[:rows].astype(BF)


COST = pl.CostEstimate(flops=1000, bytes_accessed=1000, transcendentals=0)
ANY = pl.BlockSpec(memory_space=pl.ANY)
VMEM = pl.BlockSpec(memory_space=pltpu.VMEM)


def in_hbm(arrays):
    return [pltpu.with_memory_space_constraint(x, pltpu.HBM) for x in arrays]


def in_vmem(arrays):
    return [pltpu.with_memory_space_constraint(x, pltpu.VMEM) for x in arrays]


def tie(x, *after):
    return pl.pallas_call(
        lambda *refs: None,
        in_specs=[ANY] * (1 + len(after)),
        out_specs=ANY,
        out_shape=jax.ShapeDtypeStruct(x.shape, x.dtype),
        input_output_aliases={0: 0},
        compiler_params=pltpu.CompilerParams(vmem_limit_bytes=1024 * 1024),
        cost_estimate=COST,
    )(x, *after)


def block_kernel(tokens, cotangent, ids, gates, out):
    tok, feat = tokens.shape
    out[:, :feat] = tokens[...]
    out[:, feat : 2 * feat] = cotangent[...]
    expert = lax.broadcasted_iota(jnp.int32, (LANES, tok), 0)
    table = jnp.full((LANES, tok), -1.0, F32)
    for k in range(ids.shape[0]):
        table = jnp.where(expert == ids[k : k + 1, :], gates[k : k + 1, :].astype(F32), table)
    out[:, 2 * feat :] = table.T.astype(BF)


def make_block(tokens, cotangent, ids, gates):
    tok, feat = tokens.shape
    return pl.pallas_call(
        block_kernel,
        out_shape=jax.ShapeDtypeStruct((tok, 2 * feat + LANES), BF),
        compiler_params=pltpu.CompilerParams(vmem_limit_bytes=VMEM_LIMIT),
        cost_estimate=COST,
    )(*in_hbm([tokens, cotangent, ids.T, gates.T]))


def forward_kernel(cfg, *refs):
    inner, cap, tok, feat, hid, tile, fresh, n_after, n_slabs, n_add = cfg
    refs = list(refs)

    def take(n):
        out = refs[:n]
        del refs[:n]
        return out

    blocks = take(inner)
    weights = take(3)
    take(n_after + n_slabs)
    added = take(2 if n_add else 0)
    parts, x_all, sd_all, st_out, grow_out, token = take(6)
    sums = take(n_add)
    held = take(3 if fresh else 0)
    cat, x_s, dy_s, lower, *sems = refs
    rows = inner * cap
    pad = x_s.shape[0]
    step = pl.program_id(0)
    off = pl.multiple_of(step * tile, tile)
    cols = pl.ds(off, tile)

    def fetch(i, at):
        cut = (at, slice(None)) if i == 2 else (slice(None), at)
        return pltpu.make_async_copy(weights[i].at[cut], held[i].at[cut], sems[0].at[i])

    @pl.when(step == 0)
    def _():
        if fresh:
            for i in range(3):
                fetch(i, pl.ds(0, tile)).start()
        me = lax.axis_index("expert")
        mine = (lax.broadcasted_iota(jnp.int32, (tok, LANES), 1) == me).astype(F32)
        r = lax.broadcasted_iota(jnp.int32, (tok, tok), 0)
        c = lax.broadcasted_iota(jnp.int32, (tok, tok), 1)
        lower[...] = (c < r).astype(F32).astype(BF)
        slot_of = lax.broadcasted_iota(jnp.int32, (tok, pad), 1)
        st = []
        gates = []
        for b in range(inner):
            cat[b * tok : (b + 1) * tok, :] = blocks[b][:, : 2 * feat]
            table = blocks[b][:, 2 * feat :].astype(F32)
            gate = jnp.sum(table * mine, axis=1, keepdims=True)
            chosen = gate >= 0.0
            flag = jnp.broadcast_to(chosen.astype(F32), (tok, LANES))
            before = dot(lower[...], flag.astype(BF))[:, :1]
            place = jnp.where(chosen, before.astype(jnp.int32) + b * cap, -1)
            st.append((slot_of == place).astype(F32))
            gates.append(jnp.broadcast_to(gate, (tok, LANES)).astype(BF))
        st = jnp.concatenate(st, axis=0)
        gates = jnp.concatenate(gates, axis=0)
        st_out[...] = st.astype(BF)
        pick = st.T.astype(BF)
        grow = dot(pick, gates)
        grow_out[...] = grow.astype(BF)
        x = dot(pick, cat[:, :feat]).astype(BF)
        x_s[...] = x
        x_all[...] = x
        dy = dot(pick, cat[:, feat:])
        dy_s[...] = dy.astype(BF)
        sd_all[...] = (grow[:, :1] * dy).astype(BF)
        token[...] = jnp.zeros_like(token)
        for i in range(n_add):
            sums[i][...] = (added[0][i].astype(F32) + added[1][i].astype(F32)).astype(BF)

    if fresh:
        for i in range(3):
            fetch(i, cols).wait()

        @pl.when(step + 1 < hid // tile)
        def _():
            for i in range(3):
                fetch(i, pl.ds(pl.multiple_of((step + 1) * tile, tile), tile)).start()

        weights = held
    wg, wu, wd = weights
    parts[:, cols] = dot(x_s[...], wg[:, cols])[:rows].astype(BF)
    parts[:, pl.ds(hid + off, tile)] = dot(x_s[...], wu[:, cols])[:rows].astype(BF)
    back = lax.dot_general(dy_s[...], wd[cols, :], LAST, preferred_element_type=F32)
    parts[:, pl.ds(2 * hid + off, tile)] = back[:rows].astype(BF)


def forward_call(start, total, pad, blocks, weights, fresh, cap, slabs, after, added):
    inner = len(blocks)
    tok = blocks[0].shape[0]
    feat, hid = weights[0].shape
    tile = 256 if hid % 256 == 0 else hid
    rows = inner * cap
    index = start // (inner // 2)
    whole = lambda shape: pl.BlockSpec(shape, lambda i: (0,) * len(shape))
    slab = lambda width: pl.BlockSpec((pad, width), lambda i: (index, 0))
    n_add = added[0].shape[0] if added else 0
    in_specs = [whole(b.shape) for b in blocks] + [ANY if fresh else VMEM] * 3 + [ANY] * (len(after) + len(slabs))
    args = list(blocks) + (in_hbm(weights) if fresh else in_vmem(weights)) + in_hbm(after[:1]) + list(after[1:])
    aliases = {len(args) + i: 1 + i for i in range(len(slabs))}
    args += [*slabs, *in_hbm(added[:1]), *added[1:]]
    in_specs += [whole(a.shape) for a in added]
    out_specs = [
        whole((rows, 3 * hid)),
        slab(feat),
        slab(feat),
        whole((inner * tok, pad)),
        whole((pad, LANES)),
        whole((8, LANES)),
    ]
    out_shape = [
        pltpu.HBM((rows, 3 * hid), BF),
        pltpu.HBM((total, feat), BF),
        pltpu.HBM((total, feat), BF),
        pltpu.HBM((inner * tok, pad), BF),
        pltpu.HBM((pad, LANES), BF),
        pltpu.HBM((8, LANES), F32),
    ]
    for i in range(n_add):
        out_specs.append(whole(added[0].shape[1:]))
        out_shape.append(pltpu.HBM(added[0].shape[1:], BF))
    scratch = [
        pltpu.VMEM((inner * tok, 2 * feat), BF),
        pltpu.VMEM((pad, feat), BF),
        pltpu.VMEM((pad, feat), BF),
        pltpu.VMEM((tok, tok), BF),
    ]
    if fresh:
        out_specs += [VMEM] * 3
        out_shape += [pltpu.VMEM(w.shape, w.dtype) for w in weights]
        scratch.append(pltpu.SemaphoreType.DMA((3,)))
    cfg = (inner, cap, tok, feat, hid, tile, fresh, len(after), len(slabs), n_add)
    out = pl.pallas_call(
        functools.partial(forward_kernel, cfg),
        grid=(hid // tile,),
        in_specs=in_specs,
        out_specs=out_specs,
        out_shape=out_shape,
        scratch_shapes=scratch,
        input_output_aliases=aliases,
        compiler_params=pltpu.CompilerParams(vmem_limit_bytes=VMEM_LIMIT),
        cost_estimate=COST,
    )(*args)
    return out[:6], out[6 : 6 + n_add], out[6 + n_add :]


def backward_kernel(inner, tok, feat, hid, tile, n_parts, *refs):
    parts = refs[:n_parts]
    st, grow, wg, wu = refs[n_parts : n_parts + 4]
    keep, send, act_all, pg_all, pu_all, token = refs[-8:-2]
    pg_s, pu_s = refs[-2:]
    rows = parts[0].shape[0]
    pad = pg_s.shape[0]
    half = inner // 2
    step = pl.program_id(0)

    def spread(value, column, width):
        for b in range(inner):
            piece = value[b * tok : (b + 1) * tok]
            target = keep if b % 2 == 0 else send
            target[b // 2, :, pl.ds(column, width)] = piece

    @pl.when(step == 0)
    def _():
        def total(at):
            out = parts[0][:, at * hid : (at + 1) * hid].astype(F32)
            for part in parts[1:]:
                out = out + part[:, at * hid : (at + 1) * hid].astype(F32)
            return out

        def full(value):
            if pad > rows:
                value = jnp.concatenate([value, jnp.zeros((pad - rows, value.shape[1]), F32)], axis=0)
            return value

        gate_pre = total(0)
        sig = 1.0 / (1.0 + jnp.exp(-gate_pre))
        silu = gate_pre * sig
        up = total(1)
        act = silu * up
        back = total(2)
        slot = jnp.sum(act * back, axis=1, keepdims=True)
        act_grad = grow[:rows, :1].astype(F32) * back
        pre_gate = act_grad * up * sig * (1.0 + gate_pre * (1.0 - sig))
        pre_up = act_grad * silu
        token[...] = jnp.zeros_like(token)
        act_all[...] = full(act).astype(BF)
        pg = full(pre_gate).astype(BF)
        pu = full(pre_up).astype(BF)
        pg_all[...] = pg
        pu_all[...] = pu
        pg_s[...] = pg
        pu_s[...] = pu
        me = lax.axis_index("expert")
        mine = (lax.broadcasted_iota(jnp.int32, (rows, LANES), 1) == me).astype(F32)
        slots = full(slot * mine).astype(BF)
        spread(dot(st[...], slots).astype(BF), feat, LANES)

    off = pl.multiple_of(step * tile, tile)
    cut = pl.ds(off, tile)
    grad = lax.dot_general(pg_s[...], wg[cut, :], LAST, preferred_element_type=F32)
    grad = grad + lax.dot_general(pu_s[...], wu[cut, :], LAST, preferred_element_type=F32)
    spread(dot(st[...], grad.astype(BF)).astype(BF), off, tile)


def backward_call(start, total, pad, parts, st, grow, wg, wu, tok, slabs, after):
    feat, hid = wg.shape
    tile = 512 if feat % 512 == 0 else feat
    inner = st.shape[0] // tok
    rows = parts[0].shape[0]
    index = start // (inner // 2)
    wide = feat + LANES
    whole = lambda shape: pl.BlockSpec(shape, lambda i: (0,) * len(shape))
    slab = pl.BlockSpec((pad, hid), lambda i: (index, 0))
    args = in_hbm(parts[:1]) + list(parts[1:]) + in_hbm([st, grow]) + in_vmem([wg, wu]) + in_hbm(after[:1]) + list(after[1:])
    in_specs = [whole(a.shape) for a in args[: len(parts) + 2]] + [VMEM] * 2 + [ANY] * len(after)
    aliases = {}
    if slabs:
        aliases = {len(args) + i: 2 + i for i in range(3)}
        args += list(slabs)
        in_specs += [ANY] * 3
    half = pltpu.HBM((inner // 2, tok, wide), BF)
    saved = pltpu.HBM((total, hid), BF)
    return pl.pallas_call(
        functools.partial(backward_kernel, inner, tok, feat, hid, tile, len(parts)),
        grid=(feat // tile,),
        in_specs=in_specs,
        out_specs=[whole(half.shape), whole(half.shape), slab, slab, slab, whole((8, LANES))],
        out_shape=[half, half, saved, saved, saved, pltpu.HBM((8, LANES), F32)],
        scratch_shapes=[pltpu.VMEM((pad, hid), BF), pltpu.VMEM((pad, hid), BF)],
        input_output_aliases=aliases,
        compiler_params=pltpu.CompilerParams(vmem_limit_bytes=VMEM_LIMIT),
        cost_estimate=COST,
    )(*args)


def local(tokens, cotangent, expert_ids, gate_values, gate_weight, up_weight, down_weight):
    experts = lax.axis_size("expert")
    seqs = lax.axis_size("seq")
    tok, feat = tokens.shape
    top = expert_ids.shape[1]
    cap = min(tok, tok * top // experts + tok * top // (8 * experts))
    inner = 2 * seqs if experts % (2 * seqs) == 0 else 2
    columns = inner // 2
    planes = experts // inner

    def split(i):
        return i // inner, (i % inner) // 2, i % 2

    def join(z, y, c):
        return (z % planes) * inner + (y % columns) * 2 + c

    def shift(dz=0, dy=0, dc=0):
        out = []
        for i in range(experts):
            z, y, c = split(i)
            out.append((i, join(z + dz, y + dy, c ^ dc)))
        return out

    def move(x, **by):
        return lax.ppermute(x, "expert", shift(**by))

    wg, wu, wd = gate_weight[0], up_weight[0], down_weight[0]
    hit = expert_ids[:, :, None] == jnp.arange(LANES, dtype=jnp.int32)
    block = make_block(tokens, cotangent, expert_ids, gate_values)

    def swap(part):
        if seqs == 2:
            return [part, lax.ppermute(part, "seq", [(0, 1), (1, 0)])]
        gathered = lax.all_gather(part, "seq", axis=0)
        return [gathered[i] for i in range(seqs)]

    order = list(range(planes // 2 + 1)) + list(range(planes - 1, planes // 2, -1))
    pieces = [(k, j) for k in order for j in range(columns)]
    ends = [1 + columns * i for i in range(planes)]
    ends += [ends[-1] + i for i in range(1, columns)]
    chunks = [pieces[lo:hi] for lo, hi in zip([0] + ends, ends)]
    unit = round_up(2 * cap, 16)
    total_rows = planes * columns * unit
    starts, at = [0] * len(chunks), 0
    for size in sorted({len(c) for c in chunks}, reverse=True):
        for n, chunk in enumerate(chunks):
            if len(chunk) == size:
                starts[n], at = at, at + size

    arrived = {(0, 0): block}
    pending = {}

    def send_on(k):
        own = arrived[k, 0]
        for j in range(1, columns):
            pending[k, j] = move(own, dy=j)
        if k < planes - k and k + 1 <= planes // 2:
            pending[k + 1, 0] = move(own, dz=1)
        if k == 0 and planes > 2:
            pending[planes - 1, 0] = move(own, dz=-1)
        elif planes - k < k and planes - k + 1 < (planes + 1) // 2:
            pending[k - 1, 0] = move(own, dz=-1)

    send_on(0)
    x_slab = act_slab = ()
    returned = {}

    def finish(entry, after):
        nonlocal act_slab
        start, chunk, parts, st, grow = entry
        keep, send, *act_slab, token = backward_call(
            start, total_rows, len(chunk) * unit, parts, st, grow, *held[:2], tok, act_slab, after
        )
        return token, (keep, move(send, dc=1))

    def add(keep, got):
        return [(keep[i].astype(F32) + got[i].astype(F32)).astype(BF) for i in range(keep.shape[0])]

    def give_back(chunk, sums):
        for (k, j), value in zip(chunk, sums):
            returned[k, j] = move(value, dy=-j) if j else value

    def gather_plane(k):
        return [returned[k, j] for j in range(columns)]

    def total(values):
        return sum(v.astype(F32) for v in values[1:]) + values[0].astype(F32)

    held = (wg, wu, wd)
    entries, unsent = {}, {}
    mark = None

    def arrive(piece, after):
        if piece not in arrived:
            arrived[piece] = tie(pending.pop(piece), *after)
            if piece[1] == 0:
                send_on(piece[0])

    def go_forward(n, after, added, more=()):
        nonlocal x_slab, held
        blocks = []
        for piece in chunks[n]:
            arrive(piece, after)
            blocks += [arrived[piece], move(arrived[piece], dc=1)]
        halves = unsent.pop(added, ())
        (part, *x_slab, st, grow, sent), sums, loaded = forward_call(
            starts[n], total_rows, len(chunks[n]) * unit, blocks, held, n == 0, cap, x_slab,
            [x for x in [mark, *more] if x is not None], halves
        )
        held = loaded or held
        if halves:
            give_back(chunks[added], sums)
        entries[n] = (starts[n], chunks[n], swap(part), st, grow)
        return sent

    def go_back(n, after):
        token, unsent[n] = finish(entries.pop(n), after)
        return token

    count = len(chunks)
    mark = go_forward(0, [], None)
    first = entries[0][2][1:]
    mark = go_back(0, [mark])
    mark = go_forward(1, first, None)
    for n in range(2, count):
        mark = go_forward(n, [mark], n - 2, ())
        mark = go_back(n - 1, [mark] + ([v for p, v in returned.items() if p[1]][:columns - 1] if n == count - 1 else []))
    sent_back = [v for p, v in returned.items() if p[1]]
    for n in list(unsent):
        sums = add(*unsent.pop(n))
        give_back(chunks[n], sums)
    mark = go_back(count - 1, [mark, *sums, *sent_back])
    sums = add(*unsent.pop(count - 1))
    give_back(chunks[-1], sums)

    up, down, leaving = [], [], []
    for k in range(planes // 2, 0, -1):
        leaving.append(total(gather_plane(k) + up).astype(BF))
        up = [move(leaving[-1], dz=-1)]
    for k in range(planes // 2 + 1, planes):
        leaving.append(total(gather_plane(k) + down).astype(BF))
        down = [move(leaving[-1], dz=1)]
    totals = total(gather_plane(0) + up + down)

    input_grad = totals[:, :feat].astype(BF)
    slots = totals[:, feat:]
    gate_grad = jnp.sum(jnp.where(hit, slots[:, None, :], 0.0), axis=2).astype(BF)
    contract_rows = (((0,), (0,)), ((), ()))
    wgrad = lambda a, b: lax.dot_general(a, b, contract_rows, preferred_element_type=F32).astype(BF)[None]
    x_all, sd_all = x_slab
    act_all, pg_all, pu_all = act_slab
    down_grad = wgrad(act_all, tie(sd_all, leaving[0]))
    x_all = tie(x_all, *leaving)
    gate_w_grad = wgrad(x_all, pg_all)
    up_w_grad = wgrad(x_all, pu_all)
    return (
        input_grad,
        gate_grad,
        gate_w_grad,
        up_w_grad,
        down_grad,
    )


def solution(mesh):
    in_specs = (
        P("expert", "seq"),
        P("expert", "seq"),
        P("expert", None),
        P("expert", None),
        P("expert", "seq", None),
        P("expert", "seq", None),
        P("expert", None, "seq"),
    )
    out_specs = (
        P("expert", "seq"),
        P("expert", None),
        P("expert", "seq", None),
        P("expert", "seq", None),
        P("expert", None, "seq"),
    )
    return jax.shard_map(local, mesh=mesh, in_specs=in_specs, out_specs=out_specs, check_vma=False)
```

```python
import functools

import jax
import jax.numpy as jnp
from jax import lax
from jax.experimental import pallas as pl
from jax.experimental.pallas import tpu as pltpu
from jax.sharding import PartitionSpec as P

BF = jnp.bfloat16
F32 = jnp.float32
LANES = 128
VMEM_LIMIT = 30 * 1024 * 1024
LAST = (((1,), (1,)), ((), ()))


def dot(a, b):
    return jnp.dot(a, b, preferred_element_type=F32)


def round_up(n, m):
    return -(-n // m) * m


def forward_kernel(inner, cap, tok, feat, hid, tile, *refs):
    blocks = refs[:inner]
    wg, wu, wd = refs[inner : inner + 3]
    parts, x_all, sd_all, st_out, grow_out = refs[-9:-4]
    cat, x_s, dy_s, lower = refs[-4:]
    rows = inner * cap
    pad = x_s.shape[0]
    step = pl.program_id(0)

    @pl.when(step == 0)
    def _():
        me = lax.axis_index("expert")
        mine = (lax.broadcasted_iota(jnp.int32, (tok, LANES), 1) == me).astype(F32)
        r = lax.broadcasted_iota(jnp.int32, (tok, tok), 0)
        c = lax.broadcasted_iota(jnp.int32, (tok, tok), 1)
        lower[...] = (c < r).astype(F32).astype(BF)
        slot_of = lax.broadcasted_iota(jnp.int32, (tok, pad), 1)
        st = []
        gates = []
        for b in range(inner):
            cat[b * tok : (b + 1) * tok, :] = blocks[b][:, : 2 * feat]
            table = blocks[b][:, 2 * feat :].astype(F32)
            gate = jnp.sum(table * mine, axis=1, keepdims=True)
            chosen = gate >= 0.0
            flag = jnp.broadcast_to(chosen.astype(F32), (tok, LANES))
            before = dot(lower[...], flag.astype(BF))[:, :1]
            place = jnp.where(chosen, before.astype(jnp.int32) + b * cap, -1)
            st.append((slot_of == place).astype(F32))
            gates.append(jnp.broadcast_to(gate, (tok, LANES)).astype(BF))
        st = jnp.concatenate(st, axis=0)
        gates = jnp.concatenate(gates, axis=0)
        st_out[...] = st.astype(BF)
        pick = st.T.astype(BF)
        grow = dot(pick, gates)
        grow_out[...] = grow.astype(BF)
        x = dot(pick, cat[:, :feat]).astype(BF)
        x_s[...] = x
        x_all[...] = x
        dy = dot(pick, cat[:, feat:])
        dy_s[...] = dy.astype(BF)
        sd_all[...] = (grow[:, :1] * dy).astype(BF)

    off = pl.multiple_of(step * tile, tile)
    cols = pl.ds(off, tile)
    parts[:, cols] = dot(x_s[...], wg[:, cols])[:rows].astype(BF)
    parts[:, pl.ds(hid + off, tile)] = dot(x_s[...], wu[:, cols])[:rows].astype(BF)
    back = lax.dot_general(dy_s[...], wd[cols, :], LAST, preferred_element_type=F32)
    parts[:, pl.ds(2 * hid + off, tile)] = back[:rows].astype(BF)


COST = pl.CostEstimate(flops=1000, bytes_accessed=1000, transcendentals=0)
ANY = pl.BlockSpec(memory_space=pl.ANY)
VMEM = pl.BlockSpec(memory_space=pltpu.VMEM)


def in_hbm(arrays):
    return [pltpu.with_memory_space_constraint(x, pltpu.HBM) for x in arrays]


def in_vmem(arrays):
    return [pltpu.with_memory_space_constraint(x, pltpu.VMEM) for x in arrays]


def tie(x, *after):
    return pl.pallas_call(
        lambda *refs: None,
        in_specs=[ANY] * (1 + len(after)),
        out_specs=ANY,
        out_shape=jax.ShapeDtypeStruct(x.shape, x.dtype),
        input_output_aliases={0: 0},
        compiler_params=pltpu.CompilerParams(vmem_limit_bytes=1024 * 1024),
        cost_estimate=COST,
    )(x, *[in_hbm([a])[0] if a.dtype == F32 else a for a in after])


def block_kernel(tokens, cotangent, ids, gates, out):
    tok, feat = tokens.shape
    out[:, :feat] = tokens[...]
    out[:, feat : 2 * feat] = cotangent[...]
    expert = lax.broadcasted_iota(jnp.int32, (LANES, tok), 0)
    table = jnp.full((LANES, tok), -1.0, F32)
    for k in range(ids.shape[0]):
        table = jnp.where(expert == ids[k : k + 1, :], gates[k : k + 1, :].astype(F32), table)
    out[:, 2 * feat :] = table.T.astype(BF)


def make_block(tokens, cotangent, ids, gates):
    tok, feat = tokens.shape
    return pl.pallas_call(
        block_kernel,
        out_shape=jax.ShapeDtypeStruct((tok, 2 * feat + LANES), BF),
        compiler_params=pltpu.CompilerParams(vmem_limit_bytes=VMEM_LIMIT),
        cost_estimate=COST,
    )(*in_hbm([tokens, cotangent, ids.T, gates.T]))


def forward_kernel(cfg, *refs):
    inner, cap, tok, feat, hid, tile, fresh, n_after, n_slabs, n_add = cfg
    refs = list(refs)

    def take(n):
        out = refs[:n]
        del refs[:n]
        return out

    blocks = take(inner)
    weights = take(3)
    take(n_after + n_slabs)
    added = take(2 if n_add else 0)
    parts, x_all, sd_all, st_out, grow_out, token = take(6)
    sums = take(n_add)
    held = take(3 if fresh else 0)
    cat, x_s, dy_s, lower, *sems = refs
    rows = inner * cap
    pad = x_s.shape[0]
    step = pl.program_id(0)
    off = pl.multiple_of(step * tile, tile)
    cols = pl.ds(off, tile)

    def fetch(i, at):
        cut = (at, slice(None)) if i == 2 else (slice(None), at)
        return pltpu.make_async_copy(weights[i].at[cut], held[i].at[cut], sems[0].at[i])

    @pl.when(step == 0)
    def _():
        if fresh:
            for i in range(3):
                fetch(i, pl.ds(0, tile)).start()
        me = lax.axis_index("expert")
        mine = (lax.broadcasted_iota(jnp.int32, (tok, LANES), 1) == me).astype(F32)
        r = lax.broadcasted_iota(jnp.int32, (tok, tok), 0)
        c = lax.broadcasted_iota(jnp.int32, (tok, tok), 1)
        lower[...] = (c < r).astype(F32).astype(BF)
        slot_of = lax.broadcasted_iota(jnp.int32, (tok, pad), 1)
        st = []
        gates = []
        for b in range(inner):
            cat[b * tok : (b + 1) * tok, :] = blocks[b][:, : 2 * feat]
            table = blocks[b][:, 2 * feat :].astype(F32)
            gate = jnp.sum(table * mine, axis=1, keepdims=True)
            chosen = gate >= 0.0
            flag = jnp.broadcast_to(chosen.astype(F32), (tok, LANES))
            before = dot(lower[...], flag.astype(BF))[:, :1]
            place = jnp.where(chosen, before.astype(jnp.int32) + b * cap, -1)
            st.append((slot_of == place).astype(F32))
            gates.append(jnp.broadcast_to(gate, (tok, LANES)).astype(BF))
        st = jnp.concatenate(st, axis=0)
        gates = jnp.concatenate(gates, axis=0)
        st_out[...] = st.astype(BF)
        pick = st.T.astype(BF)
        grow = dot(pick, gates)
        grow_out[...] = grow.astype(BF)
        x = dot(pick, cat[:, :feat]).astype(BF)
        x_s[...] = x
        x_all[...] = x
        dy = dot(pick, cat[:, feat:])
        dy_s[...] = dy.astype(BF)
        sd_all[...] = (grow[:, :1] * dy).astype(BF)
        token[...] = jnp.zeros_like(token)
        for i in range(n_add):
            sums[i][...] = (added[0][i].astype(F32) + added[1][i].astype(F32)).astype(BF)

    if fresh:
        for i in range(3):
            fetch(i, cols).wait()

        @pl.when(step + 1 < hid // tile)
        def _():
            for i in range(3):
                fetch(i, pl.ds(pl.multiple_of((step + 1) * tile, tile), tile)).start()

        weights = held
    wg, wu, wd = weights
    parts[:, cols] = dot(x_s[...], wg[:, cols])[:rows].astype(BF)
    parts[:, pl.ds(hid + off, tile)] = dot(x_s[...], wu[:, cols])[:rows].astype(BF)
    back = lax.dot_general(dy_s[...], wd[cols, :], LAST, preferred_element_type=F32)
    parts[:, pl.ds(2 * hid + off, tile)] = back[:rows].astype(BF)


def forward_call(start, total, pad, blocks, weights, fresh, cap, slabs, after, added):
    inner = len(blocks)
    tok = blocks[0].shape[0]
    feat, hid = weights[0].shape
    tile = 256 if hid % 256 == 0 else hid
    rows = inner * cap
    index = start // (inner // 2)
    whole = lambda shape: pl.BlockSpec(shape, lambda i: (0,) * len(shape))
    slab = lambda width: pl.BlockSpec((pad, width), lambda i: (index, 0))
    n_add = added[0].shape[0] if added else 0
    in_specs = [whole(b.shape) for b in blocks] + [ANY if fresh else VMEM] * 3 + [ANY] * (len(after) + len(slabs))
    args = list(blocks) + (in_hbm(weights) if fresh else in_vmem(weights)) + in_hbm(after[:1]) + list(after[1:])
    aliases = {len(args) + i: 1 + i for i in range(len(slabs))}
    args += [*slabs, *in_hbm(added[:1]), *added[1:]]
    in_specs += [whole(a.shape) for a in added]
    out_specs = [
        whole((rows, 3 * hid)),
        slab(feat),
        slab(feat),
        whole((inner * tok, pad)),
        whole((pad, LANES)),
        whole((8, LANES)),
    ]
    out_shape = [
        pltpu.HBM((rows, 3 * hid), BF),
        pltpu.HBM((total, feat), BF),
        pltpu.HBM((total, feat), BF),
        pltpu.HBM((inner * tok, pad), BF),
        pltpu.HBM((pad, LANES), BF),
        pltpu.HBM((8, LANES), F32),
    ]
    for i in range(n_add):
        out_specs.append(whole(added[0].shape[1:]))
        out_shape.append(pltpu.HBM(added[0].shape[1:], BF))
    scratch = [
        pltpu.VMEM((inner * tok, 2 * feat), BF),
        pltpu.VMEM((pad, feat), BF),
        pltpu.VMEM((pad, feat), BF),
        pltpu.VMEM((tok, tok), BF),
    ]
    if fresh:
        out_specs += [VMEM] * 3
        out_shape += [pltpu.VMEM(w.shape, w.dtype) for w in weights]
        scratch.append(pltpu.SemaphoreType.DMA((3,)))
    cfg = (inner, cap, tok, feat, hid, tile, fresh, len(after), len(slabs), n_add)
    out = pl.pallas_call(
        functools.partial(forward_kernel, cfg),
        grid=(hid // tile,),
        in_specs=in_specs,
        out_specs=out_specs,
        out_shape=out_shape,
        scratch_shapes=scratch,
        input_output_aliases=aliases,
        compiler_params=pltpu.CompilerParams(vmem_limit_bytes=VMEM_LIMIT),
        cost_estimate=COST,
    )(*args)
    return out[:6], out[6 : 6 + n_add], out[6 + n_add :]


def backward_kernel(inner, tok, feat, hid, tile, n_parts, *refs):
    parts = refs[:n_parts]
    st, grow, wg, wu = refs[n_parts : n_parts + 4]
    keep, send, act_all, pg_all, pu_all, token = refs[-8:-2]
    pg_s, pu_s = refs[-2:]
    rows = parts[0].shape[0]
    pad = pg_s.shape[0]
    half = inner // 2
    step = pl.program_id(0)

    def spread(value, column, width):
        for b in range(inner):
            piece = value[b * tok : (b + 1) * tok]
            target = keep if b % 2 == 0 else send
            target[b // 2, :, pl.ds(column, width)] = piece

    @pl.when(step == 0)
    def _():
        def total(at):
            out = parts[0][:, at * hid : (at + 1) * hid].astype(F32)
            for part in parts[1:]:
                out = out + part[:, at * hid : (at + 1) * hid].astype(F32)
            return out

        def full(value):
            if pad > rows:
                value = jnp.concatenate([value, jnp.zeros((pad - rows, value.shape[1]), F32)], axis=0)
            return value

        gate_pre = total(0)
        sig = 1.0 / (1.0 + jnp.exp(-gate_pre))
        silu = gate_pre * sig
        up = total(1)
        act = silu * up
        back = total(2)
        slot = jnp.sum(act * back, axis=1, keepdims=True)
        act_grad = grow[:rows, :1].astype(F32) * back
        pre_gate = act_grad * up * sig * (1.0 + gate_pre * (1.0 - sig))
        pre_up = act_grad * silu
        token[...] = jnp.zeros_like(token)
        act_all[...] = full(act).astype(BF)
        pg = full(pre_gate).astype(BF)
        pu = full(pre_up).astype(BF)
        pg_all[...] = pg
        pu_all[...] = pu
        pg_s[...] = pg
        pu_s[...] = pu
        me = lax.axis_index("expert")
        mine = (lax.broadcasted_iota(jnp.int32, (rows, LANES), 1) == me).astype(F32)
        slots = full(slot * mine).astype(BF)
        spread(dot(st[...], slots).astype(BF), feat, LANES)

    off = pl.multiple_of(step * tile, tile)
    cut = pl.ds(off, tile)
    grad = lax.dot_general(pg_s[...], wg[cut, :], LAST, preferred_element_type=F32)
    grad = grad + lax.dot_general(pu_s[...], wu[cut, :], LAST, preferred_element_type=F32)
    spread(dot(st[...], grad.astype(BF)).astype(BF), off, tile)


def backward_call(start, total, pad, parts, st, grow, wg, wu, tok, slabs, after):
    feat, hid = wg.shape
    tile = 512 if feat % 512 == 0 else feat
    inner = st.shape[0] // tok
    rows = parts[0].shape[0]
    index = start // (inner // 2)
    wide = feat + LANES
    whole = lambda shape: pl.BlockSpec(shape, lambda i: (0,) * len(shape))
    slab = pl.BlockSpec((pad, hid), lambda i: (index, 0))
    args = in_hbm(parts[:1]) + list(parts[1:]) + in_hbm([st, grow]) + in_vmem([wg, wu]) + in_hbm(after[:1]) + list(after[1:])
    in_specs = [whole(a.shape) for a in args[: len(parts) + 2]] + [VMEM] * 2 + [ANY] * len(after)
    aliases = {}
    if slabs:
        aliases = {len(args) + i: 2 + i for i in range(3)}
        args += list(slabs)
        in_specs += [ANY] * 3
    half = pltpu.HBM((inner // 2, tok, wide), BF)
    saved = pltpu.HBM((total, hid), BF)
    return pl.pallas_call(
        functools.partial(backward_kernel, inner, tok, feat, hid, tile, len(parts)),
        grid=(feat // tile,),
        in_specs=in_specs,
        out_specs=[whole(half.shape), whole(half.shape), slab, slab, slab, whole((8, LANES))],
        out_shape=[half, half, saved, saved, saved, pltpu.HBM((8, LANES), F32)],
        scratch_shapes=[pltpu.VMEM((pad, hid), BF), pltpu.VMEM((pad, hid), BF)],
        input_output_aliases=aliases,
        compiler_params=pltpu.CompilerParams(vmem_limit_bytes=VMEM_LIMIT),
        cost_estimate=COST,
    )(*args)


def local(tokens, cotangent, expert_ids, gate_values, gate_weight, up_weight, down_weight):
    experts = lax.axis_size("expert")
    seqs = lax.axis_size("seq")
    tok, feat = tokens.shape
    top = expert_ids.shape[1]
    cap = min(tok, tok * top // experts + tok * top // (8 * experts))
    inner = 2 * seqs if experts % (2 * seqs) == 0 else 2
    columns = inner // 2
    planes = experts // inner

    def split(i):
        return i // inner, (i % inner) // 2, i % 2

    def join(z, y, c):
        return (z % planes) * inner + (y % columns) * 2 + c

    def shift(dz=0, dy=0, dc=0):
        out = []
        for i in range(experts):
            z, y, c = split(i)
            out.append((i, join(z + dz, y + dy, c ^ dc)))
        return out

    def move(x, **by):
        return lax.ppermute(x, "expert", shift(**by))

    wg, wu, wd = gate_weight[0], up_weight[0], down_weight[0]
    block = make_block(tokens, cotangent, expert_ids, gate_values)

    def swap(part):
        if seqs == 2:
            return [part, lax.ppermute(part, "seq", [(0, 1), (1, 0)])]
        gathered = lax.all_gather(part, "seq", axis=0)
        return [gathered[i] for i in range(seqs)]

    order = list(range(planes // 2 + 1)) + list(range(planes - 1, planes // 2, -1))
    pieces = [(k, j) for k in order for j in range(columns)]
    ends = [1 + columns * i for i in range(planes)]
    ends += [ends[-1] + i for i in range(1, columns)]
    chunks = [pieces[lo:hi] for lo, hi in zip([0] + ends, ends)]
    unit = round_up(2 * cap, 16)
    total_rows = planes * columns * unit
    starts, at = [0] * len(chunks), 0
    for size in sorted({len(c) for c in chunks}, reverse=True):
        for n, chunk in enumerate(chunks):
            if len(chunk) == size:
                starts[n], at = at, at + size

    arrived = {(0, 0): block}
    pending = {}

    def send_on(k):
        own = arrived[k, 0]
        for j in range(1, columns):
            pending[k, j] = move(own, dy=j)
        if k < planes - k and k + 1 <= planes // 2:
            pending[k + 1, 0] = move(own, dz=1)
        if k == 0 and planes > 2:
            pending[planes - 1, 0] = move(own, dz=-1)
        elif planes - k < k and planes - k + 1 < (planes + 1) // 2:
            pending[k - 1, 0] = move(own, dz=-1)

    send_on(0)
    x_slab = act_slab = ()
    returned = {}

    def finish(entry, after):
        nonlocal act_slab
        start, chunk, parts, st, grow = entry
        keep, send, *act_slab, token = backward_call(
            start, total_rows, len(chunk) * unit, parts, st, grow, *held[:2], tok, act_slab, after
        )
        return token, (keep, move(send, dc=1))

    def add(keep, got):
        return [(keep[i].astype(F32) + got[i].astype(F32)).astype(BF) for i in range(keep.shape[0])]

    def give_back(chunk, sums):
        for (k, j), value in zip(chunk, sums):
            returned[k, j] = move(value, dy=-j) if j else value

    def gather_plane(k):
        return [returned[k, j] for j in range(columns)]

    def total(values):
        return sum(v.astype(F32) for v in values[1:]) + values[0].astype(F32)

    held = (wg, wu, wd)
    entries, unsent = {}, {}
    mark = None

    def arrive(piece, after):
        if piece not in arrived:
            arrived[piece] = tie(pending.pop(piece), *after)
            if piece[1] == 0:
                send_on(piece[0])

    def go_forward(n, after, added, more=()):
        nonlocal x_slab, held
        blocks = []
        for piece in chunks[n]:
            arrive(piece, after)
            blocks += [arrived[piece], move(arrived[piece], dc=1)]
        halves = unsent.pop(added, ())
        (part, *x_slab, st, grow, sent), sums, loaded = forward_call(
            starts[n], total_rows, len(chunks[n]) * unit, blocks, held, n == 0, cap, x_slab,
            [x for x in [mark, *more] if x is not None], halves
        )
        held = loaded or held
        if halves:
            give_back(chunks[added], sums)
        entries[n] = (starts[n], chunks[n], swap(part), st, grow)
        return sent

    def go_back(n, after):
        token, unsent[n] = finish(entries.pop(n), after)
        return token

    count = len(chunks)
    mark = go_forward(0, [], None)
    first = entries[0][2][1:]
    mark = go_back(0, [mark])
    mark = go_forward(1, first, None)
    for n in range(2, count):
        mark = go_forward(n, [mark], n - 2, ())
        mark = go_back(n - 1, [mark] + ([v for p, v in returned.items() if p[1]][:columns - 1] if n == count - 1 else []))
    sent_back = [v for p, v in returned.items() if p[1]]
    for n in list(unsent):
        sums = add(*unsent.pop(n))
        give_back(chunks[n], sums)
    mark = go_back(count - 1, [mark, *sums, *sent_back])
    sums = add(*unsent.pop(count - 1))
    give_back(chunks[-1], sums)

    up, down, leaving = [], [], []
    for k in range(planes // 2, 0, -1):
        leaving.append(total(gather_plane(k) + up).astype(BF))
        up = [move(leaving[-1], dz=-1)]
    for k in range(planes // 2 + 1, planes):
        leaving.append(total(gather_plane(k) + down).astype(BF))
        down = [move(leaving[-1], dz=1)]
    home = gather_plane(0) + up + down
    input_grad = total([v[:, :feat] for v in home]).astype(BF)
    slots = total([v[:, feat:] for v in home])
    hit = expert_ids.T[:, :, None] == jnp.arange(LANES, dtype=jnp.int32)
    gate_grad = jnp.sum(jnp.where(hit, slots[None], 0.0), axis=2).astype(BF).T
    contract_rows = (((0,), (0,)), ((), ()))
    wgrad = lambda a, b: lax.dot_general(a, b, contract_rows, preferred_element_type=F32).astype(BF)[None]
    x_all, sd_all = x_slab
    act_all, pg_all, pu_all = act_slab
    down_grad = wgrad(act_all, tie(sd_all, leaving[0]))
    x_all = tie(x_all, *leaving)
    gate_w_grad = wgrad(x_all, pg_all)
    up_w_grad = wgrad(x_all, pu_all)
    return (
        input_grad,
        gate_grad,
        gate_w_grad,
        up_w_grad,
        down_grad,
    )


def solution(mesh):
    in_specs = (
        P("expert", "seq"),
        P("expert", "seq"),
        P("expert", None),
        P("expert", None),
        P("expert", "seq", None),
        P("expert", "seq", None),
        P("expert", None, "seq"),
    )
    out_specs = (
        P("expert", "seq"),
        P("expert", None),
        P("expert", "seq", None),
        P("expert", "seq", None),
        P("expert", None, "seq"),
    )
    return jax.shard_map(local, mesh=mesh, in_specs=in_specs, out_specs=out_specs, check_vma=False)
```

```python
import functools

import jax
import jax.numpy as jnp
from jax import lax
from jax.experimental import pallas as pl
from jax.experimental.pallas import tpu as pltpu
from jax.sharding import PartitionSpec as P

BF = jnp.bfloat16
F32 = jnp.float32
LANES = 128
VMEM_LIMIT = 30 * 1024 * 1024
LAST = (((1,), (1,)), ((), ()))


def dot(a, b):
    return jnp.dot(a, b, preferred_element_type=F32)


def round_up(n, m):
    return -(-n // m) * m


def forward_kernel(inner, cap, tok, feat, hid, tile, *refs):
    blocks = refs[:inner]
    wg, wu, wd = refs[inner : inner + 3]
    parts, x_all, sd_all, st_out, grow_out = refs[-9:-4]
    cat, x_s, dy_s, lower = refs[-4:]
    rows = inner * cap
    pad = x_s.shape[0]
    step = pl.program_id(0)

    @pl.when(step == 0)
    def _():
        me = lax.axis_index("expert")
        mine = (lax.broadcasted_iota(jnp.int32, (tok, LANES), 1) == me).astype(F32)
        r = lax.broadcasted_iota(jnp.int32, (tok, tok), 0)
        c = lax.broadcasted_iota(jnp.int32, (tok, tok), 1)
        lower[...] = (c < r).astype(F32).astype(BF)
        slot_of = lax.broadcasted_iota(jnp.int32, (tok, pad), 1)
        st = []
        gates = []
        for b in range(inner):
            cat[b * tok : (b + 1) * tok, :] = blocks[b][:, : 2 * feat]
            table = blocks[b][:, 2 * feat :].astype(F32)
            gate = jnp.sum(table * mine, axis=1, keepdims=True)
            chosen = gate >= 0.0
            flag = jnp.broadcast_to(chosen.astype(F32), (tok, LANES))
            before = dot(lower[...], flag.astype(BF))[:, :1]
            place = jnp.where(chosen, before.astype(jnp.int32) + b * cap, -1)
            st.append((slot_of == place).astype(F32))
            gates.append(jnp.broadcast_to(gate, (tok, LANES)).astype(BF))
        st = jnp.concatenate(st, axis=0)
        gates = jnp.concatenate(gates, axis=0)
        st_out[...] = st.astype(BF)
        pick = st.T.astype(BF)
        grow = dot(pick, gates)
        grow_out[...] = grow.astype(BF)
        x = dot(pick, cat[:, :feat]).astype(BF)
        x_s[...] = x
        x_all[...] = x
        dy = dot(pick, cat[:, feat:])
        dy_s[...] = dy.astype(BF)
        sd_all[...] = (grow[:, :1] * dy).astype(BF)

    off = pl.multiple_of(step * tile, tile)
    cols = pl.ds(off, tile)
    parts[:, cols] = dot(x_s[...], wg[:, cols])[:rows].astype(BF)
    parts[:, pl.ds(hid + off, tile)] = dot(x_s[...], wu[:, cols])[:rows].astype(BF)
    back = lax.dot_general(dy_s[...], wd[cols, :], LAST, preferred_element_type=F32)
    parts[:, pl.ds(2 * hid + off, tile)] = back[:rows].astype(BF)


COST = pl.CostEstimate(flops=1000, bytes_accessed=1000, transcendentals=0)
ANY = pl.BlockSpec(memory_space=pl.ANY)
VMEM = pl.BlockSpec(memory_space=pltpu.VMEM)


def in_hbm(arrays):
    return [pltpu.with_memory_space_constraint(x, pltpu.HBM) for x in arrays]


def in_vmem(arrays):
    return [pltpu.with_memory_space_constraint(x, pltpu.VMEM) for x in arrays]


def tie(x, *after):
    return pl.pallas_call(
        lambda *refs: None,
        in_specs=[ANY] * (1 + len(after)),
        out_specs=ANY,
        out_shape=jax.ShapeDtypeStruct(x.shape, x.dtype),
        input_output_aliases={0: 0},
        compiler_params=pltpu.CompilerParams(vmem_limit_bytes=1024 * 1024),
        cost_estimate=COST,
    )(x, *[in_hbm([a])[0] if a.dtype == F32 else a for a in after])


def block_kernel(tokens, cotangent, ids, gates, out):
    tok, feat = tokens.shape
    out[:, :feat] = tokens[...]
    out[:, feat : 2 * feat] = cotangent[...]
    expert = lax.broadcasted_iota(jnp.int32, (LANES, tok), 0)
    table = jnp.full((LANES, tok), -1.0, F32)
    for k in range(ids.shape[0]):
        table = jnp.where(expert == ids[k : k + 1, :], gates[k : k + 1, :].astype(F32), table)
    out[:, 2 * feat :] = table.T.astype(BF)


def make_block(tokens, cotangent, ids, gates):
    tok, feat = tokens.shape
    return pl.pallas_call(
        block_kernel,
        out_shape=jax.ShapeDtypeStruct((tok, 2 * feat + LANES), BF),
        compiler_params=pltpu.CompilerParams(vmem_limit_bytes=VMEM_LIMIT),
        cost_estimate=COST,
    )(*in_hbm([tokens, cotangent, ids.T, gates.T]))


def forward_kernel(cfg, *refs):
    inner, cap, tok, feat, hid, tile, fresh, n_after, n_slabs, n_add = cfg
    refs = list(refs)

    def take(n):
        out = refs[:n]
        del refs[:n]
        return out

    blocks = take(inner)
    weights = take(3)
    take(n_after + n_slabs)
    added = take(2 if n_add else 0)
    parts, x_all, sd_all, st_out, grow_out, token = take(6)
    sums = take(n_add)
    held = take(3 if fresh else 0)
    cat, x_s, dy_s, lower, *sems = refs
    rows = inner * cap
    pad = x_s.shape[0]
    step = pl.program_id(0)
    off = pl.multiple_of(step * tile, tile)
    cols = pl.ds(off, tile)

    def fetch(i, at):
        cut = (at, slice(None)) if i == 2 else (slice(None), at)
        return pltpu.make_async_copy(weights[i].at[cut], held[i].at[cut], sems[0].at[i])

    @pl.when(step == 0)
    def _():
        if fresh:
            for i in range(3):
                fetch(i, pl.ds(0, tile)).start()
        me = lax.axis_index("expert")
        mine = (lax.broadcasted_iota(jnp.int32, (tok, LANES), 1) == me).astype(F32)
        r = lax.broadcasted_iota(jnp.int32, (tok, tok), 0)
        c = lax.broadcasted_iota(jnp.int32, (tok, tok), 1)
        lower[...] = (c < r).astype(F32).astype(BF)
        slot_of = lax.broadcasted_iota(jnp.int32, (tok, pad), 1)
        st = []
        gates = []
        for b in range(inner):
            cat[b * tok : (b + 1) * tok, :] = blocks[b][:, : 2 * feat]
            table = blocks[b][:, 2 * feat :].astype(F32)
            gate = jnp.sum(table * mine, axis=1, keepdims=True)
            chosen = gate >= 0.0
            flag = jnp.broadcast_to(chosen.astype(F32), (tok, LANES))
            before = dot(lower[...], flag.astype(BF))[:, :1]
            place = jnp.where(chosen, before.astype(jnp.int32) + b * cap, -1)
            st.append((slot_of == place).astype(F32))
            gates.append(jnp.broadcast_to(gate, (tok, LANES)).astype(BF))
        st = jnp.concatenate(st, axis=0)
        gates = jnp.concatenate(gates, axis=0)
        st_out[...] = st.astype(BF)
        pick = st.T.astype(BF)
        grow = dot(pick, gates)
        grow_out[...] = grow.astype(BF)
        x = dot(pick, cat[:, :feat]).astype(BF)
        x_s[...] = x
        x_all[...] = x
        dy = dot(pick, cat[:, feat:])
        dy_s[...] = dy.astype(BF)
        sd_all[...] = (grow[:, :1] * dy).astype(BF)
        token[...] = jnp.zeros_like(token)
        for i in range(n_add):
            sums[i][...] = (added[0][i].astype(F32) + added[1][i].astype(F32)).astype(BF)

    if fresh:
        for i in range(3):
            fetch(i, cols).wait()

        @pl.when(step + 1 < hid // tile)
        def _():
            for i in range(3):
                fetch(i, pl.ds(pl.multiple_of((step + 1) * tile, tile), tile)).start()

        weights = held
    wg, wu, wd = weights
    parts[:, cols] = dot(x_s[...], wg[:, cols])[:rows].astype(BF)
    parts[:, pl.ds(hid + off, tile)] = dot(x_s[...], wu[:, cols])[:rows].astype(BF)
    back = lax.dot_general(dy_s[...], wd[cols, :], LAST, preferred_element_type=F32)
    parts[:, pl.ds(2 * hid + off, tile)] = back[:rows].astype(BF)


def forward_call(start, total, pad, blocks, weights, fresh, cap, slabs, after, added):
    inner = len(blocks)
    tok = blocks[0].shape[0]
    feat, hid = weights[0].shape
    tile = 256 if hid % 256 == 0 else hid
    rows = inner * cap
    index = start // (inner // 2)
    whole = lambda shape: pl.BlockSpec(shape, lambda i: (0,) * len(shape))
    slab = lambda width: pl.BlockSpec((pad, width), lambda i: (index, 0))
    n_add = added[0].shape[0] if added else 0
    in_specs = [whole(b.shape) for b in blocks] + [ANY if fresh else VMEM] * 3 + [ANY] * (len(after) + len(slabs))
    args = list(blocks) + (in_hbm(weights) if fresh else in_vmem(weights)) + in_hbm(after[:1]) + list(after[1:])
    aliases = {len(args) + i: 1 + i for i in range(len(slabs))}
    args += [*slabs, *added]
    in_specs += [whole(a.shape) for a in added]
    out_specs = [
        whole((rows, 3 * hid)),
        slab(feat),
        slab(feat),
        whole((inner * tok, pad)),
        whole((pad, LANES)),
        whole((8, LANES)),
    ]
    out_shape = [
        jax.ShapeDtypeStruct((rows, 3 * hid), BF),
        pltpu.HBM((total, feat), BF),
        pltpu.HBM((total, feat), BF),
        pltpu.HBM((inner * tok, pad), BF),
        pltpu.HBM((pad, LANES), BF),
        pltpu.HBM((8, LANES), F32),
    ]
    for i in range(n_add):
        out_specs.append(whole(added[0].shape[1:]))
        out_shape.append(pltpu.HBM(added[0].shape[1:], BF))
    scratch = [
        pltpu.VMEM((inner * tok, 2 * feat), BF),
        pltpu.VMEM((pad, feat), BF),
        pltpu.VMEM((pad, feat), BF),
        pltpu.VMEM((tok, tok), BF),
    ]
    if fresh:
        out_specs += [VMEM] * 3
        out_shape += [pltpu.VMEM(w.shape, w.dtype) for w in weights]
        scratch.append(pltpu.SemaphoreType.DMA((3,)))
    cfg = (inner, cap, tok, feat, hid, tile, fresh, len(after), len(slabs), n_add)
    out = pl.pallas_call(
        functools.partial(forward_kernel, cfg),
        grid=(hid // tile,),
        in_specs=in_specs,
        out_specs=out_specs,
        out_shape=out_shape,
        scratch_shapes=scratch,
        input_output_aliases=aliases,
        compiler_params=pltpu.CompilerParams(vmem_limit_bytes=VMEM_LIMIT),
        cost_estimate=COST,
    )(*args)
    return out[:6], out[6 : 6 + n_add], out[6 + n_add :]


def backward_kernel(inner, tok, feat, hid, tile, n_parts, *refs):
    parts = refs[:n_parts]
    st, grow, wg, wu = refs[n_parts : n_parts + 4]
    keep, send, act_all, pg_all, pu_all, token = refs[-8:-2]
    pg_s, pu_s = refs[-2:]
    rows = parts[0].shape[0]
    pad = pg_s.shape[0]
    half = inner // 2
    step = pl.program_id(0)

    def spread(value, column, width):
        for b in range(inner):
            piece = value[b * tok : (b + 1) * tok]
            target = keep if b % 2 == 0 else send
            target[b // 2, :, pl.ds(column, width)] = piece

    @pl.when(step == 0)
    def _():
        def total(at):
            out = parts[0][:, at * hid : (at + 1) * hid].astype(F32)
            for part in parts[1:]:
                out = out + part[:, at * hid : (at + 1) * hid].astype(F32)
            return out

        def full(value):
            if pad > rows:
                value = jnp.concatenate([value, jnp.zeros((pad - rows, value.shape[1]), F32)], axis=0)
            return value

        gate_pre = total(0)
        sig = 1.0 / (1.0 + jnp.exp(-gate_pre))
        silu = gate_pre * sig
        up = total(1)
        act = silu * up
        back = total(2)
        slot = jnp.sum(act * back, axis=1, keepdims=True)
        act_grad = grow[:rows, :1].astype(F32) * back
        pre_gate = act_grad * up * sig * (1.0 + gate_pre * (1.0 - sig))
        pre_up = act_grad * silu
        token[...] = jnp.zeros_like(token)
        act_all[...] = full(act).astype(BF)
        pg = full(pre_gate).astype(BF)
        pu = full(pre_up).astype(BF)
        pg_all[...] = pg
        pu_all[...] = pu
        pg_s[...] = pg
        pu_s[...] = pu
        me = lax.axis_index("expert")
        mine = (lax.broadcasted_iota(jnp.int32, (rows, LANES), 1) == me).astype(F32)
        slots = full(slot * mine).astype(BF)
        spread(dot(st[...], slots).astype(BF), feat, LANES)

    off = pl.multiple_of(step * tile, tile)
    cut = pl.ds(off, tile)
    grad = lax.dot_general(pg_s[...], wg[cut, :], LAST, preferred_element_type=F32)
    grad = grad + lax.dot_general(pu_s[...], wu[cut, :], LAST, preferred_element_type=F32)
    spread(dot(st[...], grad.astype(BF)).astype(BF), off, tile)


def backward_call(start, total, pad, parts, st, grow, wg, wu, tok, slabs, after):
    feat, hid = wg.shape
    tile = 512 if feat % 512 == 0 else feat
    inner = st.shape[0] // tok
    rows = parts[0].shape[0]
    index = start // (inner // 2)
    wide = feat + LANES
    whole = lambda shape: pl.BlockSpec(shape, lambda i: (0,) * len(shape))
    slab = pl.BlockSpec((pad, hid), lambda i: (index, 0))
    args = list(parts) + in_hbm([st, grow]) + in_vmem([wg, wu]) + in_hbm(after[:1]) + list(after[1:])
    in_specs = [whole(a.shape) for a in args[: len(parts) + 2]] + [VMEM] * 2 + [ANY] * len(after)
    aliases = {}
    if slabs:
        aliases = {len(args) + i: 2 + i for i in range(3)}
        args += list(slabs)
        in_specs += [ANY] * 3
    half = jax.ShapeDtypeStruct((inner // 2, tok, wide), BF)
    saved = pltpu.HBM((total, hid), BF)
    return pl.pallas_call(
        functools.partial(backward_kernel, inner, tok, feat, hid, tile, len(parts)),
        grid=(feat // tile,),
        in_specs=in_specs,
        out_specs=[whole(half.shape), whole(half.shape), slab, slab, slab, whole((8, LANES))],
        out_shape=[half, half, saved, saved, saved, pltpu.HBM((8, LANES), F32)],
        scratch_shapes=[pltpu.VMEM((pad, hid), BF), pltpu.VMEM((pad, hid), BF)],
        input_output_aliases=aliases,
        compiler_params=pltpu.CompilerParams(vmem_limit_bytes=VMEM_LIMIT),
        cost_estimate=COST,
    )(*args)


def local(tokens, cotangent, expert_ids, gate_values, gate_weight, up_weight, down_weight):
    experts = lax.axis_size("expert")
    seqs = lax.axis_size("seq")
    tok, feat = tokens.shape
    top = expert_ids.shape[1]
    cap = min(tok, tok * top // experts + tok * top // (8 * experts))
    inner = 2 * seqs if experts % (2 * seqs) == 0 else 2
    columns = inner // 2
    planes = experts // inner

    def split(i):
        return i // inner, (i % inner) // 2, i % 2

    def join(z, y, c):
        return (z % planes) * inner + (y % columns) * 2 + c

    def shift(dz=0, dy=0, dc=0):
        out = []
        for i in range(experts):
            z, y, c = split(i)
            out.append((i, join(z + dz, y + dy, c ^ dc)))
        return out

    def move(x, **by):
        return lax.ppermute(x, "expert", shift(**by))

    wg, wu, wd = gate_weight[0], up_weight[0], down_weight[0]
    block = make_block(tokens, cotangent, expert_ids, gate_values)

    def swap(part):
        if seqs == 2:
            return [part, lax.ppermute(part, "seq", [(0, 1), (1, 0)])]
        gathered = lax.all_gather(part, "seq", axis=0)
        return [gathered[i] for i in range(seqs)]

    order = list(range(planes // 2 + 1)) + list(range(planes - 1, planes // 2, -1))
    pieces = [(k, j) for k in order for j in range(columns)]
    ends = [1 + columns * i for i in range(planes)]
    ends += [ends[-1] + i for i in range(1, columns)]
    chunks = [pieces[lo:hi] for lo, hi in zip([0] + ends, ends)]
    unit = round_up(2 * cap, 16)
    total_rows = planes * columns * unit
    starts, at = [0] * len(chunks), 0
    for size in sorted({len(c) for c in chunks}, reverse=True):
        for n, chunk in enumerate(chunks):
            if len(chunk) == size:
                starts[n], at = at, at + size

    arrived = {(0, 0): block}
    pending = {}

    def send_on(k):
        own = arrived[k, 0]
        for j in range(1, columns):
            pending[k, j] = move(own, dy=j)
        if k < planes - k and k + 1 <= planes // 2:
            pending[k + 1, 0] = move(own, dz=1)
        if k == 0 and planes > 2:
            pending[planes - 1, 0] = move(own, dz=-1)
        elif planes - k < k and planes - k + 1 < (planes + 1) // 2:
            pending[k - 1, 0] = move(own, dz=-1)

    send_on(0)
    x_slab = act_slab = ()
    returned = {}

    def finish(entry, after):
        nonlocal act_slab
        start, chunk, parts, st, grow = entry
        keep, send, *act_slab, token = backward_call(
            start, total_rows, len(chunk) * unit, parts, st, grow, *held[:2], tok, act_slab, after
        )
        return token, (keep, move(send, dc=1))

    def add(keep, got):
        return [(keep[i].astype(F32) + got[i].astype(F32)).astype(BF) for i in range(keep.shape[0])]

    def give_back(chunk, sums):
        for (k, j), value in zip(chunk, sums):
            returned[k, j] = move(value, dy=-j) if j else value

    def gather_plane(k):
        return [returned[k, j] for j in range(columns)]

    def total(values):
        return sum(v.astype(F32) for v in values[1:]) + values[0].astype(F32)

    held = (wg, wu, wd)
    entries, unsent = {}, {}
    mark = None

    def arrive(piece, after):
        if piece not in arrived:
            arrived[piece] = tie(pending.pop(piece), *after)
            if piece[1] == 0:
                send_on(piece[0])

    def go_forward(n, after, added, more=()):
        nonlocal x_slab, held
        blocks = []
        for piece in chunks[n]:
            arrive(piece, after)
            blocks += [arrived[piece], move(arrived[piece], dc=1)]
        halves = unsent.pop(added, ())
        (part, *x_slab, st, grow, sent), sums, loaded = forward_call(
            starts[n], total_rows, len(chunks[n]) * unit, blocks, held, n == 0, cap, x_slab,
            [x for x in [mark, *more] if x is not None], halves
        )
        held = loaded or held
        if halves:
            give_back(chunks[added], sums)
        entries[n] = (starts[n], chunks[n], swap(part), st, grow)
        return sent

    def go_back(n, after):
        token, unsent[n] = finish(entries.pop(n), after)
        return token

    count = len(chunks)
    mark = go_forward(0, [], None)
    first = entries[0][2][1:]
    mark = go_back(0, [mark])
    mark = go_forward(1, first, None)
    for n in range(2, count):
        mark = go_forward(n, [mark], n - 2, ())
        mark = go_back(n - 1, [mark] + ([v for p, v in returned.items() if p[1]][:columns - 1] if n == count - 1 else []))
    sent_back = [v for p, v in returned.items() if p[1]]
    for n in list(unsent):
        sums = add(*unsent.pop(n))
        give_back(chunks[n], sums)
    mark = go_back(count - 1, [mark, *sums, *sent_back])
    sums = add(*unsent.pop(count - 1))
    give_back(chunks[-1], sums)

    up, down, leaving = [], [], []
    for k in range(planes // 2, 0, -1):
        leaving.append(total(gather_plane(k) + up).astype(BF))
        up = [move(leaving[-1], dz=-1)]
    for k in range(planes // 2 + 1, planes):
        leaving.append(total(gather_plane(k) + down).astype(BF))
        down = [move(leaving[-1], dz=1)]
    home = gather_plane(0) + up + down
    input_grad = total([v[:, :feat] for v in home]).astype(BF)
    slots = total([v[:, feat:] for v in home])
    hit = expert_ids.T[:, :, None] == jnp.arange(LANES, dtype=jnp.int32)
    gate_grad = jnp.sum(jnp.where(hit, slots[None], 0.0), axis=2).astype(BF).T
    contract_rows = (((0,), (0,)), ((), ()))
    wgrad = lambda a, b: lax.dot_general(a, b, contract_rows, preferred_element_type=F32).astype(BF)[None]
    x_all, sd_all = x_slab
    act_all, pg_all, pu_all = act_slab
    down_grad = wgrad(act_all, tie(sd_all, leaving[0]))
    x_all = tie(x_all, *leaving)
    gate_w_grad = wgrad(x_all, pg_all)
    up_w_grad = wgrad(x_all, pu_all)
    return (
        input_grad,
        gate_grad,
        gate_w_grad,
        up_w_grad,
        down_grad,
    )


def solution(mesh):
    in_specs = (
        P("expert", "seq"),
        P("expert", "seq"),
        P("expert", None),
        P("expert", None),
        P("expert", "seq", None),
        P("expert", "seq", None),
        P("expert", None, "seq"),
    )
    out_specs = (
        P("expert", "seq"),
        P("expert", None),
        P("expert", "seq", None),
        P("expert", "seq", None),
        P("expert", None, "seq"),
    )
    return jax.shard_map(local, mesh=mesh, in_specs=in_specs, out_specs=out_specs, check_vma=False)
```
